128 devices in a mesh: dp: 8 (over y, core), tensor: 16 (over z, x).
Axes of the slice: x: 4, y: 4, z: 4, core: 2. Of those that a mesh axis runs over, the one named last changes fastest.
Arguments:
- tokens: bfloat16 [16384, 8192], P('dp', 'tensor'), may hold values from -6 to 6
- cotangent: bfloat16 [16384, 8192], P('dp', 'tensor'), may hold values from -6 to 6
- first_blocks: bfloat16 [32, 256, 256], P('tensor'), may hold values from -0.375 to 0.375
- second_blocks: bfloat16 [32, 256, 1024], P('tensor'), may hold values from -0.375 to 0.375
- third_blocks: bfloat16 [32, 1024, 256], P('tensor'), may hold values from -0.1875 to 0.1875
- fourth_blocks: bfloat16 [32, 256, 256], P('tensor'), may hold values from -0.375 to 0.375
Outputs:
- layer_out: bfloat16 [16384, 8192], P('dp', 'tensor')
- tokens_grad: bfloat16 [16384, 8192], P('dp', 'tensor')
- first_grad: float32 [32, 256, 256], P('tensor', 'dp')
- second_grad: float32 [32, 256, 1024], P('tensor', 'dp')
- third_grad: float32 [32, 1024, 256], P('tensor', 'dp')
- fourth_grad: float32 [32, 256, 256], P('tensor', 'dp')
The draws below stay inside these ranges and needn't reach their ends.
All inputs are finite; a program needn't handle non-finite values.
Results may differ from the reference program's by a relative error of at most 0.017.
Values may be sent and summed in bfloat16 or wider, within the bound.
A program may use at most 128 MiB of HBM per device.

```python
import math
import jax
import jax.numpy as jnp
from jax import lax

D = 8192
BLK = 256
NB = 32
HB = 1024
TOKENS = 16384


def levels(key, shape, shards, low, high):
    loudness = 1.0
    for position, parts in shards:
        draws = jax.random.uniform(jax.random.fold_in(jax.random.fold_in(key, 6), position), (parts,), jnp.float32, low / len(shards), high / len(shards))
        loudness = loudness * jnp.repeat(jnp.exp(draws), shape[position] // parts).reshape((-1,) + (1,) * (len(shape) - 1 - position))
    return loudness


def gaussian(own_key, dims, spread, reach, cuts=(), dtype=jnp.bfloat16):
    entries = spread * jax.random.normal(own_key, dims, jnp.float32)
    if cuts:
        entries = entries * levels(own_key, dims, cuts, -0.22, 0.18)
    return jnp.clip(entries, -reach, reach).astype(dtype)


def setup_inputs(seed: int = 0) -> dict:
    arg_keys = jax.random.split(jax.random.key(seed), 7)
    tokens = gaussian(arg_keys[0], (TOKENS, D), 1.0, 6.0, ((0, 8), (1, 16)))
    cotangent = gaussian(arg_keys[1], (TOKENS, D), 1.0, 6.0, ((0, 8), (1, 16)))
    first_blocks = gaussian(arg_keys[2], (NB, BLK, BLK), BLK ** -0.5, 0.375, ((0, 16),))
    second_blocks = gaussian(arg_keys[3], (NB, BLK, HB), BLK ** -0.5, 0.375, ((0, 16),))
    third_blocks = gaussian(arg_keys[4], (NB, HB, BLK), HB ** -0.5, 0.1875, ((0, 16),))
    fourth_blocks = gaussian(arg_keys[5], (NB, BLK, BLK), BLK ** -0.5, 0.375, ((0, 16),))
    return {"tokens": tokens, "cotangent": cotangent, "first_blocks": first_blocks, "second_blocks": second_blocks, "third_blocks": third_blocks, "fourth_blocks": fourth_blocks}


def reference(tokens, cotangent, first_blocks, second_blocks, third_blocks, fourth_blocks):
    sub_width = BLK // NB
    block_rows = math.gcd(TOKENS, 1024)
    scale_factor = 1.0 / math.sqrt(TOKENS)
    first_full = first_blocks.astype(jnp.float32)
    second_view = second_blocks.reshape(NB, sub_width, NB, HB).astype(jnp.float32)
    third_full = third_blocks.astype(jnp.float32)
    fourth_view = fourth_blocks.reshape(NB, sub_width, NB, BLK).astype(jnp.float32)

    def one_block(carry, pieces):
        token_piece, grad_piece = pieces
        inputs = token_piece.reshape(block_rows, NB, BLK).astype(jnp.float32)
        mixed_in = jnp.einsum('trc,rcj->trj', inputs, first_full).astype(jnp.bfloat16)
        mixed_view = mixed_in.reshape(block_rows, NB, NB, sub_width).astype(jnp.float32)
        pre_act = jnp.einsum('trks,ksro->tko', mixed_view, second_view)
        hidden = jax.nn.gelu(pre_act).astype(jnp.bfloat16).astype(jnp.float32)
        mixed_down = jnp.einsum('tko,kom->tkm', hidden, third_full).astype(jnp.bfloat16)
        down_view = mixed_down.reshape(block_rows, NB, NB, sub_width).astype(jnp.float32)
        layer_piece = jnp.einsum('tkrs,rskc->trc', down_view, fourth_view).astype(jnp.bfloat16)
        grads_in = grad_piece.reshape(block_rows, NB, BLK).astype(jnp.float32)
        back_down = jnp.einsum('trc,rskc->tkrs', grads_in, fourth_view).astype(jnp.bfloat16)
        back_down = back_down.reshape(block_rows, NB, BLK).astype(jnp.float32)
        fourth_part = jnp.einsum('tkrs,trc->rskc', down_view, grads_in).reshape(NB, BLK, BLK)
        third_part = jnp.einsum('tko,tkm->kom', hidden, back_down)
        hidden_grad = jnp.einsum('tkm,kom->tko', back_down, third_full)
        unused, pull_back = jax.vjp(jax.nn.gelu, pre_act)
        pre_grad = pull_back(hidden_grad)[0].astype(jnp.bfloat16).astype(jnp.float32)
        second_part = jnp.einsum('trks,tko->ksro', mixed_view, pre_grad).reshape(NB, BLK, HB)
        back_in = jnp.einsum('tko,ksro->trks', pre_grad, second_view).astype(jnp.bfloat16)
        back_in = back_in.reshape(block_rows, NB, BLK).astype(jnp.float32)
        first_part = jnp.einsum('trc,trj->rcj', inputs, back_in)
        input_piece = jnp.einsum('trj,rcj->trc', back_in, first_full).astype(jnp.bfloat16)
        totals = (carry[0] + first_part, carry[1] + second_part, carry[2] + third_part, carry[3] + fourth_part)
        return (totals, (layer_piece.reshape(block_rows, D), input_piece.reshape(block_rows, D)))
    start_sums = (jnp.zeros((NB, BLK, BLK), jnp.float32), jnp.zeros((NB, BLK, HB), jnp.float32), jnp.zeros((NB, HB, BLK), jnp.float32), jnp.zeros((NB, BLK, BLK), jnp.float32))
    block_count = TOKENS // block_rows
    totals, outputs = lax.scan(one_block, start_sums, (tokens.reshape(block_count, block_rows, D), cotangent.reshape(block_count, block_rows, D)))
    layer_out = outputs[0].reshape(TOKENS, D)
    tokens_grad = outputs[1].reshape(TOKENS, D)
    return (layer_out, tokens_grad, totals[0] * scale_factor, totals[1] * scale_factor, totals[2] * scale_factor, totals[3] * scale_factor)
```

```python
import functools
import math

import jax
import jax.numpy as jnp
from jax import lax
from jax.experimental import pallas as pl
from jax.experimental.pallas import tpu as pltpu
from jax.sharding import PartitionSpec as P

F32 = jnp.float32
BF16 = jnp.bfloat16
CHUNKS = 4
TILE = 128
COEF = math.sqrt(2.0 / math.pi)
CUBE = 0.044715 * COEF


def dot(a, b):
    return lax.dot_general(a, b, (((1,), (0,)), ((), ())), preferred_element_type=F32)


def dot_nt(a, b):
    return lax.dot_general(a, b, (((1,), (1,)), ((), ())), preferred_element_type=F32)


def perm_in():
    i = lax.broadcasted_iota(jnp.int32, (256, 256), 0)
    j = lax.broadcasted_iota(jnp.int32, (256, 256), 1)
    return jnp.where((i & 7) * 32 + (i >> 3) == j, 1.0, 0.0).astype(BF16)


def perm_out():
    i = lax.broadcasted_iota(jnp.int32, (256, 256), 0)
    j = lax.broadcasted_iota(jnp.int32, (256, 256), 1)
    return jnp.where((i & 31) * 8 + (i >> 5) == j, 1.0, 0.0).astype(BF16)


def pack(dst, c, a, b):
    for q in range(16):
        lo = q * 16
        rows = [a[lo:lo + 8], b[lo:lo + 8], a[lo + 8:lo + 16], b[lo + 8:lo + 16]]
        dst[c, q] = jnp.concatenate(rows, axis=0).astype(BF16)


def kernel(scale,
           x_hbm, g_hbm, w1_hbm, w2_hbm, w3_hbm, w4_hbm,
           lo_hbm, tg_hbm, g1_hbm, g2_hbm, g3_hbm, g4_hbm,
           x, g, w1, w2, w3, w4, w1t, w2p, w2t, w3t, w4p,
           s1, s2, s3, s4, r1, r2, r3, r4, hid, pgr, md, bi,
           a1, a2, a3, a4, q1, q2, q3, q4, p1, p2, p3, p4,
           lo, tg, o1, o2, o3, o4,
           wsem, xsem, gsem, ssem, rsem, qsem, psem, osem):
    T = x.shape[0] // CHUNKS
    dp = lax.axis_index("dp")
    me = lax.axis_index("tensor")
    mz, mx = me // 4, me % 4

    def rows_of(c):
        return pl.ds(pl.multiple_of(c * T, T), T)

    loads = [
        pltpu.make_async_copy(h, v, wsem.at[i])
        for i, (h, v) in enumerate([(w1_hbm, w1), (w4_hbm, w4), (w2_hbm, w2), (w3_hbm, w3)])
    ]

    def load_x(c):
        return pltpu.make_async_copy(x_hbm.at[rows_of(c)], x.at[rows_of(c)], xsem.at[c])

    def load_g(c):
        return pltpu.make_async_copy(g_hbm.at[rows_of(c)], g.at[rows_of(c)], gsem.at[c])

    loads[0].start()
    load_x(0).start()
    loads[1].start()
    load_g(0).start()
    for c in range(1, CHUNKS):
        load_x(c).start()
        load_g(c).start()
    loads[2].start()
    loads[3].start()

    barrier = pltpu.get_barrier_semaphore()

    def greet_tensor(i, carry):
        pl.semaphore_signal(barrier, inc=1, device_id={"tensor": (me + i) % 16})
        return carry

    def greet_dp(i, carry):
        pl.semaphore_signal(barrier, inc=1, device_id={"dp": (dp + i) % 8})
        return carry

    lax.fori_loop(1, 16, greet_tensor, 0)
    lax.fori_loop(1, 8, greet_dp, 0)

    def send(n, src, dst, c):
        def one(i, carry):
            q = ((mz + i // 4) % 4) * 4 + (mx + i % 4) % 4
            pltpu.make_async_remote_copy(
                src_ref=src.at[c, q], dst_ref=dst.at[c, me],
                send_sem=ssem.at[n, c], recv_sem=rsem.at[n, c],
                device_id={"tensor": q},
            ).start()
            return carry

        pltpu.make_async_copy(src.at[c, me], dst.at[c, me], rsem.at[n, c]).start()
        lax.fori_loop(1, 16, one, 0)

    def arrive(n, dst, c):
        pltpu.make_async_copy(dst.at[c], dst.at[c], rsem.at[n, c]).wait()

    def sent(n, src, c):
        part = src.at[c, pl.ds(0, 15)]
        pltpu.make_async_copy(part, part, ssem.at[n, c]).wait()

    loads[0].wait()
    for b in range(2):
        w1t[b] = w1[b].T
    loads[1].wait()
    pin = perm_in()
    for b in range(2):
        w4p[b] = dot(pin, w4[b]).astype(BF16)

    pl.semaphore_wait(barrier, 22)

    def mix(c, carry):
        load_x(c).wait()
        a, b = (dot_nt(w1t[n], x[rows_of(c), n * 256:(n + 1) * 256]) for n in range(2))
        pack(s1, c, a, b)
        send(0, s1, r1, c)
        load_g(c).wait()
        a, b = (dot_nt(w4p[n], g[rows_of(c), n * 256:(n + 1) * 256]) for n in range(2))
        pack(s2, c, a, b)
        send(1, s2, r2, c)
        return carry

    lax.fori_loop(0, CHUNKS, mix, 0)

    loads[2].wait()
    loads[3].wait()
    for b in range(2):
        w2p[b] = dot(pin, w2[b]).astype(BF16)
        w2t[b] = w2p[b].T
        w3t[b] = w3[b].T
    a1[...] = jnp.zeros_like(a1)
    a2[...] = jnp.zeros_like(a2)
    a3[...] = jnp.zeros_like(a3)
    a4[...] = jnp.zeros_like(a4)

    def hidden_stage(c, carry):
        arrive(0, r1, c)
        arrive(1, r2, c)
        for k in range(2):
            arr = r1[c, :, k * 16:(k + 1) * 16, :].reshape(256, T)
            bd = r2[c, :, k * 16:(k + 1) * 16, :].reshape(256, T)

            def tile(n, inner):
                o = pl.ds(pl.multiple_of(n * TILE, TILE), TILE)
                v = dot(w2t[k, o, :], arr)
                hg = dot(w3[k, o, :], bd)
                v2 = v * v
                t = jnp.tanh(v * (COEF + CUBE * v2))
                h = 0.5 + 0.5 * t
                hid[o, :] = (v * h).astype(BF16)
                slope = h + (0.5 * v) * (1.0 - t * t) * (COEF + (3.0 * CUBE) * v2)
                pgr[o, :] = (slope * hg).astype(BF16)
                return inner

            lax.fori_loop(0, 1024 // TILE, tile, 0)
            md[k] = dot(w3t[k], hid[...])
            bi[k] = dot(w2p[k], pgr[...])
            a3[k] += dot_nt(hid[...], bd)
            a2[k] += dot_nt(pgr[...], arr)
        pack(s3, c, md[0], md[1])
        send(2, s3, r3, c)
        pack(s4, c, bi[0], bi[1])
        return carry

    lax.fori_loop(0, CHUNKS, hidden_stage, 0)

    def send_back(c, carry):
        send(3, s4, r4, c)
        return carry

    lax.fori_loop(0, CHUNKS, send_back, 0)

    def reduce_send(n, src, dst):
        def one(i, carry):
            p = (dp + i) % 8
            pltpu.make_async_remote_copy(
                src_ref=src.at[p], dst_ref=dst.at[dp],
                send_sem=qsem.at[n], recv_sem=psem.at[n],
                device_id={"dp": p},
            ).start()
            return carry

        pltpu.make_async_copy(src.at[dp], dst.at[dp], psem.at[n]).start()
        lax.fori_loop(1, 8, one, 0)

    def reduce_take(n, dst, out, out_hbm):
        pltpu.make_async_copy(dst, dst, psem.at[n]).wait()
        total = dst[0].astype(F32)
        for p in range(1, 8):
            total += dst[p].astype(F32)
        out[...] = total
        pltpu.make_async_copy(out, out_hbm, osem.at[n]).start()

    pout = perm_out()
    for k in range(2):
        for d in range(8):
            q3[d, k] = (a3[k, d * 128:(d + 1) * 128, :] * scale).astype(BF16)
    reduce_send(2, q3, p3)
    for k in range(2):
        full = dot_nt(pout, (a2[k] * scale).astype(BF16)).astype(BF16)
        for d in range(8):
            q2[d, k] = full[d * 32:(d + 1) * 32, :]
    reduce_send(1, q2, p2)

    def out_stage(c, carry):
        arrive(2, r3, c)
        rows = rows_of(c)
        for n in range(2):
            cols = slice(n * 256, (n + 1) * 256)
            ret = r3[c, :, n * 16:(n + 1) * 16, :].reshape(256, T)
            a4[n] += dot(ret, g[rows, cols])
            lo[rows, cols] = dot(ret.T, w4p[n]).astype(BF16)
        pltpu.make_async_copy(lo.at[rows], lo_hbm.at[rows], osem.at[4]).start()
        return carry

    lax.fori_loop(0, CHUNKS, out_stage, 0)
    for n in range(2):
        full = dot(pout, (a4[n] * scale).astype(BF16)).astype(BF16)
        for d in range(8):
            q4[d, n] = full[d * 32:(d + 1) * 32, :]
    reduce_send(3, q4, p4)
    reduce_take(2, p3, o3, g3_hbm)
    reduce_take(1, p2, o2, g2_hbm)

    def in_grads(c, carry):
        arrive(3, r4, c)
        rows = rows_of(c)
        for n in range(2):
            cols = slice(n * 256, (n + 1) * 256)
            ret = r4[c, :, n * 16:(n + 1) * 16, :].reshape(256, T)
            a1[n] += dot(ret, x[rows, cols])
            tg[rows, cols] = dot(ret.T, w1t[n]).astype(BF16)
        pltpu.make_async_copy(tg.at[rows], tg_hbm.at[rows], osem.at[5]).start()
        return carry

    lax.fori_loop(0, CHUNKS, in_grads, 0)
    for n in range(2):
        full = (a1[n] * scale).T.astype(BF16)
        for d in range(8):
            q1[d, n] = full[d * 32:(d + 1) * 32, :]
    reduce_send(0, q1, p1)
    reduce_take(3, p4, o4, g4_hbm)

    def drain(c, carry):
        for n, src in enumerate((s1, s2, s3, s4)):
            sent(n, src, c)
        return carry

    lax.fori_loop(0, CHUNKS, drain, 0)
    for n, src in enumerate((q1, q2, q3, q4)):
        if n:
            part = src.at[pl.ds(0, 7)]
            pltpu.make_async_copy(part, part, qsem.at[n]).wait()
    reduce_take(0, p1, o1, g1_hbm)
    part = q1.at[pl.ds(0, 7)]
    pltpu.make_async_copy(part, part, qsem.at[0]).wait()
    for n, (v, h) in enumerate([(o1, g1_hbm), (o2, g2_hbm), (o3, g3_hbm), (o4, g4_hbm), (lo, lo_hbm), (tg, tg_hbm)]):
        pltpu.make_async_copy(v, h, osem.at[n]).wait()


def shards(scale, tokens, cotangent, first, second, third, fourth):
    rows = tokens.shape[0]
    T = rows // CHUNKS
    slots = pltpu.VMEM((CHUNKS, 16, 32, T), BF16)
    any_spec = pl.BlockSpec(memory_space=pl.ANY)
    shape = jax.ShapeDtypeStruct
    grads = [(2, 32, 256), (2, 32, 1024), (2, 128, 256), (2, 32, 256)]
    return pl.pallas_call(
        functools.partial(kernel, scale),
        out_shape=[shape(tokens.shape, BF16), shape(tokens.shape, BF16)] + [shape(s, F32) for s in grads],
        in_specs=[any_spec] * 6,
        out_specs=[any_spec] * 6,
        scratch_shapes=[
            pltpu.VMEM(tokens.shape, BF16),
            pltpu.VMEM(tokens.shape, BF16),
            pltpu.VMEM(first.shape, BF16),
            pltpu.VMEM(second.shape, BF16),
            pltpu.VMEM(third.shape, BF16),
            pltpu.VMEM(fourth.shape, BF16),
            pltpu.VMEM((2, 256, 256), BF16),
            pltpu.VMEM((2, 256, 1024), BF16),
            pltpu.VMEM((2, 1024, 256), BF16),
            pltpu.VMEM((2, 256, 1024), BF16),
            pltpu.VMEM((2, 256, 256), BF16),
            slots, slots, slots, slots, slots, slots, slots, slots,
            pltpu.VMEM((1024, T), BF16),
            pltpu.VMEM((1024, T), BF16),
            pltpu.VMEM((2, 256, T), F32),
            pltpu.VMEM((2, 256, T), F32),
            pltpu.VMEM((2, 256, 256), F32),
            pltpu.VMEM((2, 1024, 256), F32),
            pltpu.VMEM((2, 1024, 256), F32),
            pltpu.VMEM((2, 256, 256), F32),
        ]
        + [pltpu.VMEM((8,) + s, BF16) for s in grads] * 2
        + [
            pltpu.VMEM(tokens.shape, BF16),
            pltpu.VMEM(tokens.shape, BF16),
        ]
        + [pltpu.VMEM(s, F32) for s in grads]
        + [
            pltpu.SemaphoreType.DMA((4,)),
            pltpu.SemaphoreType.DMA((CHUNKS,)),
            pltpu.SemaphoreType.DMA((CHUNKS,)),
            pltpu.SemaphoreType.DMA((4, CHUNKS)),
            pltpu.SemaphoreType.DMA((4, CHUNKS)),
            pltpu.SemaphoreType.DMA((4,)),
            pltpu.SemaphoreType.DMA((4,)),
            pltpu.SemaphoreType.DMA((6,)),
        ],
        compiler_params=pltpu.CompilerParams(
            collective_id=0, has_side_effects=True, vmem_limit_bytes=60 * 1024 * 1024
        ),
        cost_estimate=pl.CostEstimate(
            flops=16 * 10**9, bytes_accessed=12 * 2**20, transcendentals=4 * 2**20
        ),
    )(tokens, cotangent, first, second, third, fourth)


def solution(mesh):
    in_specs = (P("dp", "tensor"),) * 2 + (P("tensor", None, None),) * 4
    out_specs = (P("dp", "tensor"),) * 2 + (P("tensor", "dp", None),) * 4

    def run(tokens, *rest):
        scale = tokens.shape[0] ** -0.5
        step = jax.shard_map(
            functools.partial(shards, scale), mesh=mesh, in_specs=in_specs, out_specs=out_specs, check_vma=False
        )
        return step(tokens, *rest)

    return run
```

```python
import functools
import math

import jax
import jax.numpy as jnp
from jax import lax
from jax.experimental import pallas as pl
from jax.experimental.pallas import tpu as pltpu
from jax.sharding import PartitionSpec as P

F32 = jnp.float32
BF16 = jnp.bfloat16
CHUNKS = 4
TILE = 128
ORDER = ((2, 2), (1, 0), (3, 0), (2, 1), (0, 3), (1, 2), (3, 1), (0, 2), (2, 3), (1, 1), (3, 2), (0, 1), (1, 3), (2, 0), (3, 3))
COEF = math.sqrt(2.0 / math.pi)
CUBE = 0.044715 * COEF


def dot(a, b):
    return lax.dot_general(a, b, (((1,), (0,)), ((), ())), preferred_element_type=F32)


def dot_nt(a, b):
    return lax.dot_general(a, b, (((1,), (1,)), ((), ())), preferred_element_type=F32)


def perm_in():
    i = lax.broadcasted_iota(jnp.int32, (256, 256), 0)
    j = lax.broadcasted_iota(jnp.int32, (256, 256), 1)
    return jnp.where((i & 7) * 32 + (i >> 3) == j, 1.0, 0.0).astype(BF16)


def perm_out():
    i = lax.broadcasted_iota(jnp.int32, (256, 256), 0)
    j = lax.broadcasted_iota(jnp.int32, (256, 256), 1)
    return jnp.where((i & 31) * 8 + (i >> 5) == j, 1.0, 0.0).astype(BF16)


def pack(slot, a, b):
    for q in range(16):
        lo = q * 16
        rows = [a[lo:lo + 8], b[lo:lo + 8], a[lo + 8:lo + 16], b[lo + 8:lo + 16]]
        slot(q)[...] = jnp.concatenate(rows, axis=0).astype(BF16)


def kernel(scale,
           x_hbm, g_hbm, w1_hbm, w2_hbm, w3_hbm, w4_hbm,
           lo, tg, o1, o2, o3, o4,
           x, g, w1, w2, w3, w4, w1t, w2p, w2t, w3t, w4p, xt,
           s_in, r_in, s_md, r_md, s_bi, r_bi, s_end, r_end, hid, pgr, md, bi,
           a1, a2, a3, a4, q1, q2, q3, q4, p1, p2, p3, p4,
           wsem, xsem, gsem, in_sem, md_sem, bi_sem, end_sem, qsem, psem):
    T = x.shape[0] // CHUNKS
    dp = lax.axis_index("dp")
    me = lax.axis_index("tensor")
    mz, mx = me // 4, me % 4
    core = dp % 2
    turn = 1 - 2 * core

    def rows_of(c):
        return pl.ds(pl.multiple_of(c * T, T), T)

    loads = [
        pltpu.make_async_copy(h, v, wsem.at[i])
        for i, (h, v) in enumerate([(w1_hbm, w1), (w4_hbm, w4), (w2_hbm, w2), (w3_hbm, w3)])
    ]

    def load_x(c):
        return pltpu.make_async_copy(x_hbm.at[rows_of(c)], x.at[rows_of(c)], xsem.at[c])

    def load_g(c):
        return pltpu.make_async_copy(g_hbm.at[rows_of(c)], g.at[rows_of(c)], gsem.at[c])

    loads[0].start()
    load_x(0).start()
    loads[1].start()
    load_g(0).start()

    barrier = pltpu.get_barrier_semaphore()

    def greet_tensor(i, carry):
        pl.semaphore_signal(barrier, inc=1, device_id={"tensor": (me + i) % 16})
        return carry

    def greet_dp(i, carry):
        pl.semaphore_signal(barrier, inc=1, device_id={"dp": (dp + i) % 8})
        return carry

    lax.fori_loop(1, 16, greet_tensor, 0)
    lax.fori_loop(1, 8, greet_dp, 0)
    for c in range(1, CHUNKS):
        load_x(c).start()
        load_g(c).start()
    loads[2].start()
    loads[3].start()

    def send(sems, view, src, dst):
        pltpu.make_async_copy(view(src, me), view(dst, me), sems.at[1]).start()
        for dx, dz in ORDER:
            ax = (dx + core * (dz - dx)) * turn
            az = (dz + core * (dx - dz)) * turn
            q = ((mz + az + 4) % 4) * 4 + (mx + ax + 4) % 4
            pltpu.make_async_remote_copy(
                src_ref=view(src, q), dst_ref=view(dst, me),
                send_sem=sems.at[0], recv_sem=sems.at[1],
                device_id={"tensor": q},
            ).start()

    def arrive(sems, dst):
        pltpu.make_async_copy(dst, dst, sems.at[1]).wait()

    def sent(sems, src):
        part = src.at[pl.ds(0, 15)]
        pltpu.make_async_copy(part, part, sems.at[0]).wait()

    def mix_x(c):
        load_x(c).wait()
        a, b = (dot_nt(w1t[n], x[rows_of(c), n * 256:(n + 1) * 256]) for n in range(2))
        pack(lambda q: s_in.at[c, q, 0], a, b)

    def mix_g(c):
        load_g(c).wait()
        a, b = (dot_nt(w4p[n], g[rows_of(c), n * 256:(n + 1) * 256]) for n in range(2))
        pack(lambda q: s_in.at[c, q, 1], a, b)

    loads[0].wait()
    for b in range(2):
        w1t[b] = w1[b].T
    mix_x(0)
    pl.semaphore_wait(barrier, 22)
    send(in_sem.at[0], lambda ref, q: ref.at[0, q, 0], s_in, r_in)
    loads[1].wait()
    pin = perm_in()
    for b in range(2):
        w4p[b] = dot(pin, w4[b]).astype(BF16)
    mix_g(0)
    send(in_sem.at[0], lambda ref, q: ref.at[0, q, 1], s_in, r_in)

    def mix(c, carry):
        mix_x(c)
        mix_g(c)
        send(in_sem.at[c], lambda ref, q: ref.at[c, q], s_in, r_in)
        return carry

    lax.fori_loop(1, CHUNKS, mix, 0)

    loads[2].wait()
    loads[3].wait()
    for b in range(2):
        w2p[b] = dot(pin, w2[b]).astype(BF16)
        w2t[b] = w2p[b].T
        w3t[b] = w3[b].T
    a1[...] = jnp.zeros_like(a1)
    a2[...] = jnp.zeros_like(a2)
    a3[...] = jnp.zeros_like(a3)
    a4[...] = jnp.zeros_like(a4)

    def hidden_stage(c, pair):
        arrive(in_sem.at[c], r_in.at[c])
        for k in range(2):
            arr = r_in[c, :, 0, k * 16:(k + 1) * 16, :].reshape(256, T)
            bd = r_in[c, :, 1, k * 16:(k + 1) * 16, :].reshape(256, T)

            def tile(n, inner):
                o = pl.ds(pl.multiple_of(n * TILE, TILE), TILE)
                v = dot(w2t[k, o, :], arr)
                hg = dot(w3[k, o, :], bd)
                v2 = v * v
                t = jnp.tanh(v * (COEF + CUBE * v2))
                h = 0.5 + 0.5 * t
                hid[o, :] = (v * h).astype(BF16)
                slope = h + (0.5 * v) * (1.0 - t * t) * (COEF + (3.0 * CUBE) * v2)
                pgr[o, :] = (slope * hg).astype(BF16)
                return inner

            lax.fori_loop(0, 1024 // TILE, tile, 0)
            md[k] = dot(w3t[k], hid[...])
            bi[k] = dot(w2p[k], pgr[...])
            a3[k] += dot_nt(hid[...], bd)
            a2[k] += dot_nt(pgr[...], arr)
        half = c % 2
        pack(lambda q: s_md.at[pair, q, half], md[0], md[1])

        @pl.when(pair == 0)
        def _():
            pack(lambda q: s_bi.at[q, half], bi[0], bi[1])

        @pl.when(pair == 1)
        def _():
            pack(lambda q: s_end.at[half, q], bi[0], bi[1])

        return pair

    def hidden_pair(pair, carry):
        lax.fori_loop(2 * pair, 2 * pair + 2, hidden_stage, pair)
        send(md_sem.at[pair], lambda ref, q: ref.at[pair, q], s_md, r_md)

        @pl.when(pair == 0)
        def _():
            send(bi_sem, lambda ref, q: ref.at[q], s_bi, r_bi)

        return carry

    lax.fori_loop(0, 2, hidden_pair, 0)
    for half in range(2):
        send(end_sem.at[half], lambda ref, q: ref.at[half, q], s_end, r_end)

    def reduce_send(n, src, dst):
        def one(i, carry):
            p = (dp + i) % 8
            pltpu.make_async_remote_copy(
                src_ref=src.at[p], dst_ref=dst.at[dp],
                send_sem=qsem.at[n], recv_sem=psem.at[n],
                device_id={"dp": p},
            ).start()
            return carry

        pltpu.make_async_copy(src.at[dp], dst.at[dp], psem.at[n]).start()
        lax.fori_loop(1, 8, one, 0)

    def reduce_sent(n, src):
        part = src.at[pl.ds(0, 7)]
        pltpu.make_async_copy(part, part, qsem.at[n]).wait()

    def reduce_take(n, dst, out):
        pltpu.make_async_copy(dst, dst, psem.at[n]).wait()
        total = dst[0].astype(F32)
        for p in range(1, 8):
            total += dst[p].astype(F32)
        out[...] = total

    pout = perm_out()
    for k in range(2):
        for d in range(8):
            q3[d, k] = (a3[k, d * 128:(d + 1) * 128, :] * scale).astype(BF16)
    reduce_send(2, q3, p3)
    for k in range(2):
        full = dot_nt(pout, (a2[k] * scale).astype(BF16)).astype(BF16)
        for d in range(8):
            q2[d, k] = full[d * 32:(d + 1) * 32, :]
    reduce_send(1, q2, p2)

    def turn_x(c, carry):
        for n in range(2):
            xt[c, n] = x[rows_of(c), n * 256:(n + 1) * 256].T
        return carry

    lax.fori_loop(0, CHUNKS, turn_x, 0)

    def out_stage(c, pair):
        rows = rows_of(c)
        for n in range(2):
            cols = slice(n * 256, (n + 1) * 256)
            ret = r_md[pair, :, c % 2, n * 16:(n + 1) * 16, :].reshape(256, T)
            a4[n] += dot(ret, g[rows, cols])
            lo[rows, cols] = dot(ret.T, w4p[n]).astype(BF16)
        return pair

    def first_part(c, n, ret):
        a1[n] += dot_nt(xt[c, n], ret)

    def tokens_part(c, n, ret):
        tg[rows_of(c), n * 256:(n + 1) * 256] = dot(ret.T, w1t[n]).astype(BF16)

    def in_stage(c, carry):
        for n in range(2):
            ret = r_bi[:, c, n * 16:(n + 1) * 16, :].reshape(256, T)
            first_part(c, n, ret)
            tokens_part(c, n, ret)
        return carry

    arrive(md_sem.at[0], r_md.at[0])
    lax.fori_loop(0, 2, out_stage, 0)
    arrive(bi_sem, r_bi)
    lax.fori_loop(0, 2, in_stage, 0)
    reduce_take(2, p3, o3)
    reduce_take(1, p2, o2)
    arrive(md_sem.at[1], r_md.at[1])
    lax.fori_loop(2, 4, out_stage, 1)
    for n in range(2):
        full = dot(pout, (a4[n] * scale).astype(BF16)).astype(BF16)
        for d in range(8):
            q4[d, n] = full[d * 32:(d + 1) * 32, :]
    reduce_send(3, q4, p4)

    def ended(half, n):
        return r_end[half, :, n * 16:(n + 1) * 16, :].reshape(256, T)

    arrive(end_sem.at[0], r_end.at[0])
    for n in range(2):
        first_part(2, n, ended(0, n))
        tokens_part(2, n, ended(0, n))
    reduce_take(3, p4, o4)
    arrive(end_sem.at[1], r_end.at[1])
    for n in range(2):
        full = ((a1[n] + dot_nt(xt[3, n], ended(1, n))) * scale).astype(BF16)
        for d in range(8):
            q1[d, n] = full[d * 32:(d + 1) * 32, :]
    reduce_send(0, q1, p1)
    for n in range(2):
        tokens_part(3, n, ended(1, n))

    for c in range(CHUNKS):
        sent(in_sem.at[c], s_in.at[c])
    for pair in range(2):
        sent(md_sem.at[pair], s_md.at[pair])
        sent(end_sem.at[pair], s_end.at[pair])
    sent(bi_sem, s_bi)
    for n, src in enumerate((q1, q2, q3, q4)):
        reduce_sent(n, src)
    reduce_take(0, p1, o1)


def finish(*refs):
    sems = refs[-1]
    copies = [pltpu.make_async_copy(refs[n], refs[n + 6], sems.at[n]) for n in range(6)]
    for copy in copies:
        copy.start()
    for copy in copies:
        copy.wait()


def shards(scale, tokens, cotangent, first, second, third, fourth):
    rows = tokens.shape[0]
    T = rows // CHUNKS
    any_spec = pl.BlockSpec(memory_space=pl.ANY)
    shape = jax.ShapeDtypeStruct
    grads = [(2, 32, 256), (2, 32, 1024), (2, 128, 256), (2, 32, 256)]
    outs = [(tokens.shape, BF16), (tokens.shape, BF16)] + [(s, F32) for s in grads]
    parts = pl.pallas_call(
        functools.partial(kernel, scale),
        out_shape=[pltpu.VMEM(s, d) for s, d in outs],
        in_specs=[any_spec] * 6,
        out_specs=[pl.BlockSpec(memory_space=pltpu.VMEM)] * 6,
        scratch_shapes=[
            pltpu.VMEM(tokens.shape, BF16),
            pltpu.VMEM(tokens.shape, BF16),
            pltpu.VMEM(first.shape, BF16),
            pltpu.VMEM(second.shape, BF16),
            pltpu.VMEM(third.shape, BF16),
            pltpu.VMEM(fourth.shape, BF16),
            pltpu.VMEM((2, 256, 256), BF16),
            pltpu.VMEM((2, 256, 1024), BF16),
            pltpu.VMEM((2, 1024, 256), BF16),
            pltpu.VMEM((2, 256, 1024), BF16),
            pltpu.VMEM((2, 256, 256), BF16),
            pltpu.VMEM((CHUNKS, 2, 256, T), BF16),
            pltpu.VMEM((CHUNKS, 16, 2, 32, T), BF16),
            pltpu.VMEM((CHUNKS, 16, 2, 32, T), BF16),
            pltpu.VMEM((2, 16, 2, 32, T), BF16),
            pltpu.VMEM((2, 16, 2, 32, T), BF16),
            pltpu.VMEM((16, 2, 32, T), BF16),
            pltpu.VMEM((16, 2, 32, T), BF16),
            pltpu.VMEM((2, 16, 32, T), BF16),
            pltpu.VMEM((2, 16, 32, T), BF16),
            pltpu.VMEM((1024, T), BF16),
            pltpu.VMEM((1024, T), BF16),
            pltpu.VMEM((2, 256, T), F32),
            pltpu.VMEM((2, 256, T), F32),
            pltpu.VMEM((2, 256, 256), F32),
            pltpu.VMEM((2, 1024, 256), F32),
            pltpu.VMEM((2, 1024, 256), F32),
            pltpu.VMEM((2, 256, 256), F32),
        ]
        + [pltpu.VMEM((8,) + s, BF16) for s in grads] * 2
        + [
            pltpu.SemaphoreType.DMA((4,)),
            pltpu.SemaphoreType.DMA((CHUNKS,)),
            pltpu.SemaphoreType.DMA((CHUNKS,)),
            pltpu.SemaphoreType.DMA((CHUNKS, 2)),
            pltpu.SemaphoreType.DMA((2, 2)),
            pltpu.SemaphoreType.DMA((2,)),
            pltpu.SemaphoreType.DMA((2, 2)),
            pltpu.SemaphoreType.DMA((4,)),
            pltpu.SemaphoreType.DMA((4,)),
        ],
        compiler_params=pltpu.CompilerParams(
            collective_id=0, has_side_effects=True, vmem_limit_bytes=48 * 1024 * 1024
        ),
        cost_estimate=pl.CostEstimate(
            flops=16 * 10**9, bytes_accessed=12 * 2**20, transcendentals=4 * 2**20
        ),
    )(*(pltpu.with_memory_space_constraint(a, pltpu.HBM) for a in (tokens, cotangent, first, second, third, fourth)))
    return pl.pallas_call(
        finish,
        out_shape=[shape(s, d) for s, d in outs],
        in_specs=[pl.BlockSpec(memory_space=pltpu.VMEM)] * 6,
        out_specs=[any_spec] * 6,
        scratch_shapes=[pltpu.SemaphoreType.DMA((6,))],
        compiler_params=pltpu.CompilerParams(vmem_limit_bytes=1024 * 1024),
    )(*parts)


def solution(mesh):
    in_specs = (P("dp", "tensor"),) * 2 + (P("tensor", None, None),) * 4
    out_specs = (P("dp", "tensor"),) * 2 + (P("tensor", "dp", None),) * 4

    def run(tokens, *rest):
        scale = tokens.shape[0] ** -0.5
        step = jax.shard_map(
            functools.partial(shards, scale), mesh=mesh, in_specs=in_specs, out_specs=out_specs, check_vma=False
        )
        return step(tokens, *rest)

    return run
```

```python
import functools
import math

import jax
import jax.numpy as jnp
from jax import lax
from jax.experimental import pallas as pl
from jax.experimental.pallas import tpu as pltpu
from jax.sharding import PartitionSpec as P

F32 = jnp.float32
BF16 = jnp.bfloat16
CHUNKS = 4
TILE = 128
FAR = ((2, 2), (2, 1), (2, 3), (1, 2), (3, 2), (0, 2), (2, 0), (1, 1), (3, 3), (1, 3), (3, 1), (1, 0), (3, 0), (0, 1), (0, 3))
COEF = math.sqrt(2.0 / math.pi)
CUBE = 0.044715 * COEF


def dot(a, b):
    return lax.dot_general(a, b, (((1,), (0,)), ((), ())), preferred_element_type=F32)


def dot_nt(a, b):
    return lax.dot_general(a, b, (((1,), (1,)), ((), ())), preferred_element_type=F32)


def perm_in():
    i = lax.broadcasted_iota(jnp.int32, (256, 256), 0)
    j = lax.broadcasted_iota(jnp.int32, (256, 256), 1)
    return jnp.where((i & 7) * 32 + (i >> 3) == j, 1.0, 0.0).astype(BF16)


def perm_out():
    i = lax.broadcasted_iota(jnp.int32, (256, 256), 0)
    j = lax.broadcasted_iota(jnp.int32, (256, 256), 1)
    return jnp.where((i & 31) * 8 + (i >> 5) == j, 1.0, 0.0).astype(BF16)


def pack(slot, a, b):
    for q in range(16):
        lo = q * 16
        rows = [a[lo:lo + 8], b[lo:lo + 8], a[lo + 8:lo + 16], b[lo + 8:lo + 16]]
        slot(q)[...] = jnp.concatenate(rows, axis=0).astype(BF16)


def kernel(scale,
           x_hbm, g_hbm, w1_hbm, w2_hbm, w3_hbm, w4_hbm,
           lo, tg, o1, o2, o3, o4,
           x, g, w1, w2, w3, w4, w1t, w2p, w2t, w3t, w4p, xt,
           s_in, r_in, s_md, r_md, s_b0, r_b0, s_b1, r_b1, hid, pgr, md, bi,
           a1, a2, a3, a4, q0, q1, q2, q3, q4, p0, p1, p2, p3, p4,
           wsem, xsem, gsem, in_sem, md_sem, b0_sem, b1_sem, qsem, psem):
    T = x.shape[0] // CHUNKS
    dp = lax.axis_index("dp")
    me = lax.axis_index("tensor")
    mz, mx = me // 4, me % 4
    core = dp % 2
    turn = 1 - 2 * core

    def rows_of(c):
        return pl.ds(pl.multiple_of(c * T, T), T)

    loads = [
        pltpu.make_async_copy(h, v, wsem.at[i])
        for i, (h, v) in enumerate([(w1_hbm, w1), (w4_hbm, w4), (w2_hbm, w2), (w3_hbm, w3)])
    ]

    def load_x(c):
        return pltpu.make_async_copy(x_hbm.at[rows_of(c)], x.at[rows_of(c)], xsem.at[c])

    def load_g(c):
        return pltpu.make_async_copy(g_hbm.at[rows_of(c)], g.at[rows_of(c)], gsem.at[c])

    loads[0].start()
    load_x(0).start()
    loads[1].start()
    load_g(0).start()

    barrier = pltpu.get_barrier_semaphore()

    def greet_tensor(i, carry):
        pl.semaphore_signal(barrier, inc=1, device_id={"tensor": (me + i) % 16})
        return carry

    def greet_dp(i, carry):
        pl.semaphore_signal(barrier, inc=1, device_id={"dp": (dp + i) % 8})
        return carry

    lax.fori_loop(1, 16, greet_tensor, 0)
    lax.fori_loop(1, 8, greet_dp, 0)
    for c in range(1, CHUNKS):
        load_x(c).start()
        load_g(c).start()
    loads[2].start()
    loads[3].start()

    def send(sems, view, src, dst):
        pltpu.make_async_copy(view(src, me), view(dst, me), sems.at[1]).start()
        for dx, dz in FAR:
            ax = (dx + core * (dz - dx)) * turn
            az = (dz + core * (dx - dz)) * turn
            q = ((mz + az + 4) % 4) * 4 + (mx + ax + 4) % 4
            pltpu.make_async_remote_copy(
                src_ref=view(src, q), dst_ref=view(dst, me),
                send_sem=sems.at[0], recv_sem=sems.at[1],
                device_id={"tensor": q},
            ).start()

    def arrive(sems, dst):
        pltpu.make_async_copy(dst, dst, sems.at[1]).wait()

    def sent(sems, src):
        part = src.at[pl.ds(0, 15)]
        pltpu.make_async_copy(part, part, sems.at[0]).wait()

    def mix_x(c):
        load_x(c).wait()
        a, b = (dot_nt(w1t[n], x[rows_of(c), n * 256:(n + 1) * 256]) for n in range(2))
        pack(lambda q: s_in.at[c, q, 0], a, b)

    def mix_g(c):
        load_g(c).wait()
        a, b = (dot_nt(w4p[n], g[rows_of(c), n * 256:(n + 1) * 256]) for n in range(2))
        pack(lambda q: s_in.at[c, q, 1], a, b)

    loads[0].wait()
    for b in range(2):
        w1t[b] = w1[b].T
    mix_x(0)
    pl.semaphore_wait(barrier, 22)
    send(in_sem.at[0], lambda ref, q: ref.at[0, q, 0], s_in, r_in)
    loads[1].wait()
    pin = perm_in()
    for b in range(2):
        w4p[b] = dot(pin, w4[b]).astype(BF16)
    mix_g(0)
    send(in_sem.at[0], lambda ref, q: ref.at[0, q, 1], s_in, r_in)

    def mix(c, carry):
        mix_x(c)
        mix_g(c)
        send(in_sem.at[c], lambda ref, q: ref.at[c, q], s_in, r_in)
        return carry

    lax.fori_loop(1, CHUNKS, mix, 0)

    loads[2].wait()
    loads[3].wait()
    for b in range(2):
        w2p[b] = dot(pin, w2[b]).astype(BF16)
        w2t[b] = w2p[b].T
        w3t[b] = w3[b].T
    a1[...] = jnp.zeros_like(a1)
    a2[...] = jnp.zeros_like(a2)
    a3[...] = jnp.zeros_like(a3)
    a4[...] = jnp.zeros_like(a4)

    def hidden_stage(c, pair):
        arrive(in_sem.at[c], r_in.at[c])
        for k in range(2):
            arr = r_in[c, :, 0, k * 16:(k + 1) * 16, :].reshape(256, T)
            bd = r_in[c, :, 1, k * 16:(k + 1) * 16, :].reshape(256, T)

            def tile(n, inner):
                o = pl.ds(pl.multiple_of(n * TILE, TILE), TILE)
                v = dot(w2t[k, o, :], arr)
                hg = dot(w3[k, o, :], bd)
                v2 = v * v
                t = jnp.tanh(v * (COEF + CUBE * v2))
                h = 0.5 + 0.5 * t
                hid[o, :] = (v * h).astype(BF16)
                slope = h + (0.5 * v) * (1.0 - t * t) * (COEF + (3.0 * CUBE) * v2)
                pgr[o, :] = (slope * hg).astype(BF16)
                return inner

            lax.fori_loop(0, 1024 // TILE, tile, 0)
            md[k] = dot(w3t[k], hid[...])
            bi[k] = dot(w2p[k], pgr[...])
            a3[k] += dot_nt(hid[...], bd)
            a2[k] += dot_nt(pgr[...], arr)
        half = c % 2
        pack(lambda q: s_md.at[pair, q, half], md[0], md[1])

        for q in range(16):
            for n, dst in enumerate((s_b0, s_b1)):
                low = q * 16 + n * 8
                rows = [bi[0, low:low + 8], bi[1, low:low + 8]]
                dst[pair, q, half] = jnp.concatenate(rows, axis=0).astype(BF16)
        return pair

    def hidden_pair(pair, carry):
        lax.fori_loop(2 * pair, 2 * pair + 2, hidden_stage, pair)
        send(md_sem.at[pair], lambda ref, q: ref.at[pair, q], s_md, r_md)
        send(b0_sem.at[pair], lambda ref, q: ref.at[pair, q], s_b0, r_b0)
        return carry

    lax.fori_loop(0, 2, hidden_pair, 0)
    for pair in range(2):
        send(b1_sem.at[pair], lambda ref, q: ref.at[pair, q], s_b1, r_b1)

    def reduce_send(n, src, dst):
        def one(i, carry):
            p = (dp + i) % 8
            pltpu.make_async_remote_copy(
                src_ref=src.at[p], dst_ref=dst.at[dp],
                send_sem=qsem.at[n], recv_sem=psem.at[n],
                device_id={"dp": p},
            ).start()
            return carry

        lax.fori_loop(1, 8, one, 0)
        pltpu.make_async_copy(src.at[dp], dst.at[dp], psem.at[n]).start()

    def reduce_sent(n, src):
        part = src.at[pl.ds(0, 7)]
        pltpu.make_async_copy(part, part, qsem.at[n]).wait()

    def reduce_take(n, dst, out):
        pltpu.make_async_copy(dst, dst, psem.at[n]).wait()
        total = dst[0].astype(F32)
        for p in range(1, 8):
            total += dst[p].astype(F32)
        out[...] = total

    pout = perm_out()
    for k in range(2):
        for d in range(8):
            q3[d, k] = (a3[k, d * 128:(d + 1) * 128, :] * scale).astype(BF16)
    reduce_send(2, q3, p3)
    for k in range(2):
        full = dot_nt(pout, (a2[k] * scale).astype(BF16)).astype(BF16)
        for d in range(8):
            q2[d, k] = full[d * 32:(d + 1) * 32, :]
    reduce_send(1, q2, p2)

    def turn_x(c, carry):
        for n in range(2):
            xt[c, n] = x[rows_of(c), n * 256:(n + 1) * 256].T
        return carry

    lax.fori_loop(0, CHUNKS, turn_x, 0)

    def out_stage(c, pair):
        rows = rows_of(c)
        for n in range(2):
            cols = slice(n * 256, (n + 1) * 256)
            ret = r_md[pair, :, c % 2, n * 16:(n + 1) * 16, :].reshape(256, T)
            a4[n] += dot(ret, g[rows, cols])
            lo[rows, cols] = dot(ret.T, w4p[n]).astype(BF16)
        return pair

    def first_part(c, n, ret):
        a1[n] += dot_nt(xt[c, n], ret)

    def tokens_part(c, n, ret):
        tg[rows_of(c), n * 256:(n + 1) * 256] = dot(ret.T, w1t[n]).astype(BF16)

    def back(r_b, c):
        return r_b[c // 2, :, c % 2].reshape(256, T)

    def in_stage(c, carry):
        ret = back(r_b0, c)
        first_part(c, 0, ret)
        tokens_part(c, 0, ret)
        return carry

    arrive(md_sem.at[0], r_md.at[0])
    lax.fori_loop(0, 2, out_stage, 0)
    arrive(b0_sem.at[0], r_b0.at[0])
    lax.fori_loop(0, 2, in_stage, 0)
    reduce_take(2, p3, o3)
    reduce_take(1, p2, o2)
    arrive(md_sem.at[1], r_md.at[1])
    lax.fori_loop(2, 4, out_stage, 1)
    for n in range(2):
        full = dot(pout, (a4[n] * scale).astype(BF16)).astype(BF16)
        for d in range(8):
            q4[d, n] = full[d * 32:(d + 1) * 32, :]
    reduce_send(3, q4, p4)
    arrive(b0_sem.at[1], r_b0.at[1])
    lax.fori_loop(2, 4, in_stage, 0)
    full = (a1[0] * scale).astype(BF16)
    for d in range(8):
        q0[d] = full[d * 32:(d + 1) * 32, :]
    reduce_send(4, q0, p0)
    arrive(b1_sem.at[0], r_b1.at[0])
    for c in range(2):
        first_part(c, 1, back(r_b1, c))
        tokens_part(c, 1, back(r_b1, c))
    reduce_take(3, p4, o4)
    reduce_take(4, p0, o1.at[0])
    arrive(b1_sem.at[1], r_b1.at[1])
    full = a1[1] + dot_nt(xt[2, 1], back(r_b1, 2)) + dot_nt(xt[3, 1], back(r_b1, 3))
    full = (full * scale).astype(BF16)
    for d in range(8):
        q1[d] = full[d * 32:(d + 1) * 32, :]
    reduce_send(0, q1, p1)
    for c in range(2, 4):
        tokens_part(c, 1, back(r_b1, c))
    for c in range(CHUNKS):
        sent(in_sem.at[c], s_in.at[c])
    for pair in range(2):
        sent(md_sem.at[pair], s_md.at[pair])
        sent(b0_sem.at[pair], s_b0.at[pair])
        sent(b1_sem.at[pair], s_b1.at[pair])
    for n, src in enumerate((q1, q2, q3, q4, q0)):
        reduce_sent(n, src)
    reduce_take(0, p1, o1.at[1])


def finish(*refs):
    sems = refs[-1]
    copies = [pltpu.make_async_copy(refs[n], refs[n + 6], sems.at[n]) for n in range(6)]
    for copy in copies:
        copy.start()
    for copy in copies:
        copy.wait()


def shards(scale, tokens, cotangent, first, second, third, fourth):
    rows = tokens.shape[0]
    T = rows // CHUNKS
    any_spec = pl.BlockSpec(memory_space=pl.ANY)
    shape = jax.ShapeDtypeStruct
    grads = [(2, 32, 256), (2, 32, 1024), (2, 128, 256), (2, 32, 256)]
    sums = [(32, 256), (32, 256)] + grads[1:]
    outs = [(tokens.shape, BF16), (tokens.shape, BF16)] + [(s, F32) for s in grads]
    parts = pl.pallas_call(
        functools.partial(kernel, scale),
        out_shape=[pltpu.VMEM(s, d) for s, d in outs],
        in_specs=[any_spec] * 6,
        out_specs=[pl.BlockSpec(memory_space=pltpu.VMEM)] * 6,
        scratch_shapes=[
            pltpu.VMEM(tokens.shape, BF16),
            pltpu.VMEM(tokens.shape, BF16),
            pltpu.VMEM(first.shape, BF16),
            pltpu.VMEM(second.shape, BF16),
            pltpu.VMEM(third.shape, BF16),
            pltpu.VMEM(fourth.shape, BF16),
            pltpu.VMEM((2, 256, 256), BF16),
            pltpu.VMEM((2, 256, 1024), BF16),
            pltpu.VMEM((2, 1024, 256), BF16),
            pltpu.VMEM((2, 256, 1024), BF16),
            pltpu.VMEM((2, 256, 256), BF16),
            pltpu.VMEM((CHUNKS, 2, 256, T), BF16),
            pltpu.VMEM((CHUNKS, 16, 2, 32, T), BF16),
            pltpu.VMEM((CHUNKS, 16, 2, 32, T), BF16),
            pltpu.VMEM((2, 16, 2, 32, T), BF16),
            pltpu.VMEM((2, 16, 2, 32, T), BF16),
            pltpu.VMEM((2, 16, 2, 16, T), BF16),
            pltpu.VMEM((2, 16, 2, 16, T), BF16),
            pltpu.VMEM((2, 16, 2, 16, T), BF16),
            pltpu.VMEM((2, 16, 2, 16, T), BF16),
            pltpu.VMEM((1024, T), BF16),
            pltpu.VMEM((1024, T), BF16),
            pltpu.VMEM((2, 256, T), F32),
            pltpu.VMEM((2, 256, T), F32),
            pltpu.VMEM((2, 256, 256), F32),
            pltpu.VMEM((2, 1024, 256), F32),
            pltpu.VMEM((2, 1024, 256), F32),
            pltpu.VMEM((2, 256, 256), F32),
        ]
        + [pltpu.VMEM((8,) + s, BF16) for s in sums] * 2
        + [
            pltpu.SemaphoreType.DMA((4,)),
            pltpu.SemaphoreType.DMA((CHUNKS,)),
            pltpu.SemaphoreType.DMA((CHUNKS,)),
            pltpu.SemaphoreType.DMA((CHUNKS, 2)),
            pltpu.SemaphoreType.DMA((2, 2)),
            pltpu.SemaphoreType.DMA((2, 2)),
            pltpu.SemaphoreType.DMA((2, 2)),
            pltpu.SemaphoreType.DMA((5,)),
            pltpu.SemaphoreType.DMA((5,)),
        ],
        compiler_params=pltpu.CompilerParams(
            collective_id=0, has_side_effects=True, vmem_limit_bytes=48 * 1024 * 1024
        ),
        cost_estimate=pl.CostEstimate(
            flops=16 * 10**9, bytes_accessed=12 * 2**20, transcendentals=4 * 2**20
        ),
    )(*(pltpu.with_memory_space_constraint(a, pltpu.HBM) for a in (tokens, cotangent, first, second, third, fourth)))
    return pl.pallas_call(
        finish,
        out_shape=[shape(s, d) for s, d in outs],
        in_specs=[pl.BlockSpec(memory_space=pltpu.VMEM)] * 6,
        out_specs=[any_spec] * 6,
        scratch_shapes=[pltpu.SemaphoreType.DMA((6,))],
        compiler_params=pltpu.CompilerParams(vmem_limit_bytes=1024 * 1024),
    )(*parts)


def solution(mesh):
    in_specs = (P("dp", "tensor"),) * 2 + (P("tensor", None, None),) * 4
    out_specs = (P("dp", "tensor"),) * 2 + (P("tensor", "dp", None),) * 4

    def run(tokens, *rest):
        scale = tokens.shape[0] ** -0.5
        step = jax.shard_map(
            functools.partial(shards, scale), mesh=mesh, in_specs=in_specs, out_specs=out_specs, check_vma=False
        )
        return step(tokens, *rest)

    return run
```

```python
import functools
import math

import jax
import jax.numpy as jnp
from jax import lax
from jax.experimental import pallas as pl
from jax.experimental.pallas import tpu as pltpu
from jax.sharding import PartitionSpec as P

F32 = jnp.float32
BF16 = jnp.bfloat16
CHUNKS = 4
TILE = 128
FAR = ((2, 2), (2, 1), (2, 3), (1, 2), (3, 2), (0, 2), (2, 0), (1, 1), (3, 3), (1, 3), (3, 1), (1, 0), (3, 0), (0, 1), (0, 3))
ROWS = ((2, 1), (2, 0), (1, 1), (3, 1), (1, 0), (3, 0), (0, 1))
COEF = math.sqrt(2.0 / math.pi)
CUBE = 0.044715 * COEF


def dot(a, b):
    return lax.dot_general(a, b, (((1,), (0,)), ((), ())), preferred_element_type=F32)


def dot_nt(a, b):
    return lax.dot_general(a, b, (((1,), (1,)), ((), ())), preferred_element_type=F32)


def perm_in():
    i = lax.broadcasted_iota(jnp.int32, (256, 256), 0)
    j = lax.broadcasted_iota(jnp.int32, (256, 256), 1)
    return jnp.where((i & 7) * 32 + (i >> 3) == j, 1.0, 0.0).astype(BF16)


def perm_out():
    i = lax.broadcasted_iota(jnp.int32, (256, 256), 0)
    j = lax.broadcasted_iota(jnp.int32, (256, 256), 1)
    return jnp.where((i & 31) * 8 + (i >> 5) == j, 1.0, 0.0).astype(BF16)


def pack(slot, a, b):
    for q in range(16):
        lo = q * 16
        rows = [a[lo:lo + 8], b[lo:lo + 8], a[lo + 8:lo + 16], b[lo + 8:lo + 16]]
        slot(q)[...] = jnp.concatenate(rows, axis=0).astype(BF16)


def kernel(scale,
           x_hbm, g_hbm, w1_hbm, w2_hbm, w3_hbm, w4_hbm,
           lo, tg, o1, o2, o3, o4,
           x, g, w1, w2, w3, w4, w1t, w2p, w2t, w3t, w4p, xt,
           s_in, r_in, s_md, r_md, s_b0, r_b0, s_b1, r_b1, hid, pgr, md, bi,
           a1, a2, a3, a4, q0, q1, q2, q3, q4, p0, p1, p2, p3, p4,
           wsem, xsem, gsem, in_sem, md_sem, b0_sem, b1_sem, qsem, psem):
    T = x.shape[0] // CHUNKS
    dp = lax.axis_index("dp")
    me = lax.axis_index("tensor")
    mz, mx = me // 4, me % 4
    core = dp % 2
    turn = 1 - 2 * core

    def rows_of(c):
        return pl.ds(pl.multiple_of(c * T, T), T)

    loads = [
        pltpu.make_async_copy(h, v, wsem.at[i])
        for i, (h, v) in enumerate([(w1_hbm, w1), (w4_hbm, w4), (w2_hbm, w2), (w3_hbm, w3)])
    ]

    def load_x(c):
        return pltpu.make_async_copy(x_hbm.at[rows_of(c)], x.at[rows_of(c)], xsem.at[c])

    def load_g(c):
        return pltpu.make_async_copy(g_hbm.at[rows_of(c)], g.at[rows_of(c)], gsem.at[c])

    def peer(dx, dz):
        return {"tensor": ((mz + dz) % 4) * 4 + (mx + dx) % 4}

    def other(dy, dc):
        return {"dp": ((dp // 2 + dy) % 4) * 2 + (core + dc) % 2}

    barrier = pltpu.get_barrier_semaphore()
    for dx, dz in FAR:
        pl.semaphore_signal(barrier, inc=1, device_id=peer(dx, dz))
    for dy, dc in ROWS:
        pl.semaphore_signal(barrier, inc=1, device_id=other(dy, dc))
    loads[0].start()
    load_x(0).start()
    loads[1].start()
    load_g(0).start()
    for c in range(1, CHUNKS):
        load_x(c).start()
        load_g(c).start()
    loads[2].start()
    loads[3].start()

    def send(sems, view, src, dst):
        pltpu.make_async_copy(view(src, me), view(dst, me), sems.at[1]).start()
        for dx, dz in FAR:
            ax = (dx + core * (dz - dx)) * turn
            az = (dz + core * (dx - dz)) * turn
            q = ((mz + az + 4) % 4) * 4 + (mx + ax + 4) % 4
            pltpu.make_async_remote_copy(
                src_ref=view(src, q), dst_ref=view(dst, me),
                send_sem=sems.at[0], recv_sem=sems.at[1],
                device_id={"tensor": q},
            ).start()

    def arrive(sems, dst):
        pltpu.make_async_copy(dst, dst, sems.at[1]).wait()

    def sent(sems, src):
        part = src.at[pl.ds(0, 15)]
        pltpu.make_async_copy(part, part, sems.at[0]).wait()

    def mix_x(c):
        load_x(c).wait()
        a, b = (dot_nt(w1t[n], x[rows_of(c), n * 256:(n + 1) * 256]) for n in range(2))
        pack(lambda q: s_in.at[c, q, 0], a, b)

    def mix_g(c):
        load_g(c).wait()
        a, b = (dot_nt(w4p[n], g[rows_of(c), n * 256:(n + 1) * 256]) for n in range(2))
        pack(lambda q: s_in.at[c, q, 1], a, b)

    loads[0].wait()
    for b in range(2):
        w1t[b] = w1[b].T
    mix_x(0)
    pl.semaphore_wait(barrier, 22)
    send(in_sem.at[0], lambda ref, q: ref.at[0, q, 0], s_in, r_in)
    loads[1].wait()
    pin = perm_in()
    for b in range(2):
        w4p[b] = dot(pin, w4[b]).astype(BF16)
    mix_g(0)
    send(in_sem.at[0], lambda ref, q: ref.at[0, q, 1], s_in, r_in)

    def mix(c, carry):
        mix_x(c)
        mix_g(c)
        send(in_sem.at[c], lambda ref, q: ref.at[c, q], s_in, r_in)
        return carry

    lax.fori_loop(1, CHUNKS, mix, 0)

    loads[2].wait()
    loads[3].wait()
    for b in range(2):
        w2p[b] = dot(pin, w2[b]).astype(BF16)
        w2t[b] = w2p[b].T
        w3t[b] = w3[b].T
    a1[...] = jnp.zeros_like(a1)
    a2[...] = jnp.zeros_like(a2)
    a3[...] = jnp.zeros_like(a3)
    a4[...] = jnp.zeros_like(a4)

    def hidden_stage(c, pair):
        arrive(in_sem.at[c], r_in.at[c])
        for k in range(2):
            arr = r_in[c, :, 0, k * 16:(k + 1) * 16, :].reshape(256, T)
            bd = r_in[c, :, 1, k * 16:(k + 1) * 16, :].reshape(256, T)

            def tile(n, inner):
                o = pl.ds(pl.multiple_of(n * TILE, TILE), TILE)
                v = dot(w2t[k, o, :], arr)
                hg = dot(w3[k, o, :], bd)
                v2 = v * v
                t = jnp.tanh(v * (COEF + CUBE * v2))
                h = 0.5 + 0.5 * t
                hid[o, :] = (v * h).astype(BF16)
                slope = h + (0.5 * v) * (1.0 - t * t) * (COEF + (3.0 * CUBE) * v2)
                pgr[o, :] = (slope * hg).astype(BF16)
                return inner

            lax.fori_loop(0, 1024 // TILE, tile, 0)
            md[k] = dot(w3t[k], hid[...])
            bi[k] = dot(w2p[k], pgr[...])
            a3[k] += dot_nt(hid[...], bd)
            a2[k] += dot_nt(pgr[...], arr)
        half = c % 2
        pack(lambda q: s_md.at[pair, q, half], md[0], md[1])

        for q in range(16):
            for n, dst in enumerate((s_b0, s_b1)):
                low = q * 16 + n * 8
                rows = [bi[0, low:low + 8], bi[1, low:low + 8]]
                dst[pair, q, half] = jnp.concatenate(rows, axis=0).astype(BF16)
        return pair

    def hidden_pair(pair, carry):
        lax.fori_loop(2 * pair, 2 * pair + 2, hidden_stage, pair)
        send(md_sem.at[pair], lambda ref, q: ref.at[pair, q], s_md, r_md)
        send(b0_sem.at[pair], lambda ref, q: ref.at[pair, q], s_b0, r_b0)
        return carry

    lax.fori_loop(0, 2, hidden_pair, 0)
    for pair in range(2):
        send(b1_sem.at[pair], lambda ref, q: ref.at[pair, q], s_b1, r_b1)

    def reduce_send(n, src, dst):
        for dy, dc in ROWS:
            p = other(dy, dc)
            pltpu.make_async_remote_copy(
                src_ref=src.at[p["dp"]], dst_ref=dst.at[dp],
                send_sem=qsem.at[n], recv_sem=psem.at[n],
                device_id=p,
            ).start()
        pltpu.make_async_copy(src.at[dp], dst.at[dp], psem.at[n]).start()

    def reduce_sent(n, src):
        part = src.at[pl.ds(0, 7)]
        pltpu.make_async_copy(part, part, qsem.at[n]).wait()

    def reduce_take(n, dst, out):
        pltpu.make_async_copy(dst, dst, psem.at[n]).wait()
        total = dst[0].astype(F32)
        for p in range(1, 8):
            total += dst[p].astype(F32)
        out[...] = total

    pout = perm_out()
    for k in range(2):
        for d in range(8):
            q3[d, k] = (a3[k, d * 128:(d + 1) * 128, :] * scale).astype(BF16)
    reduce_send(2, q3, p3)
    for k in range(2):
        full = dot_nt(pout, (a2[k] * scale).astype(BF16)).astype(BF16)
        for d in range(8):
            q2[d, k] = full[d * 32:(d + 1) * 32, :]
    reduce_send(1, q2, p2)

    def turn_x(c, carry):
        for n in range(2):
            xt[c, n] = x[rows_of(c), n * 256:(n + 1) * 256].T
        return carry

    lax.fori_loop(0, CHUNKS, turn_x, 0)

    def out_stage(c, pair):
        rows = rows_of(c)
        for n in range(2):
            cols = slice(n * 256, (n + 1) * 256)
            ret = r_md[pair, :, c % 2, n * 16:(n + 1) * 16, :].reshape(256, T)
            a4[n] += dot(ret, g[rows, cols])
            lo[rows, cols] = dot(ret.T, w4p[n]).astype(BF16)
        return pair

    def first_part(c, n, ret):
        a1[n] += dot_nt(xt[c, n], ret)

    def tokens_part(c, n, ret):
        tg[rows_of(c), n * 256:(n + 1) * 256] = dot(ret.T, w1t[n]).astype(BF16)

    def back(r_b, c):
        return r_b[c // 2, :, c % 2].reshape(256, T)

    def in_stage(c, carry):
        ret = back(r_b0, c)
        first_part(c, 0, ret)
        tokens_part(c, 0, ret)
        return carry

    arrive(md_sem.at[0], r_md.at[0])
    lax.fori_loop(0, 2, out_stage, 0)
    arrive(b0_sem.at[0], r_b0.at[0])
    lax.fori_loop(0, 2, in_stage, 0)
    reduce_take(2, p3, o3)
    reduce_take(1, p2, o2)
    arrive(md_sem.at[1], r_md.at[1])
    lax.fori_loop(2, 4, out_stage, 1)
    for n in range(2):
        full = dot(pout, (a4[n] * scale).astype(BF16)).astype(BF16)
        for d in range(8):
            q4[d, n] = full[d * 32:(d + 1) * 32, :]
    reduce_send(3, q4, p4)
    arrive(b0_sem.at[1], r_b0.at[1])
    lax.fori_loop(2, 4, in_stage, 0)
    full = (a1[0] * scale).astype(BF16)
    for d in range(8):
        q0[d] = full[d * 32:(d + 1) * 32, :]
    reduce_send(4, q0, p0)
    arrive(b1_sem.at[0], r_b1.at[0])
    for c in range(2):
        first_part(c, 1, back(r_b1, c))
        tokens_part(c, 1, back(r_b1, c))
    reduce_take(3, p4, o4)
    reduce_take(4, p0, o1.at[0])
    arrive(b1_sem.at[1], r_b1.at[1])
    full = a1[1] + dot_nt(xt[2, 1], back(r_b1, 2)) + dot_nt(xt[3, 1], back(r_b1, 3))
    full = (full * scale).astype(BF16)
    for d in range(8):
        q1[d] = full[d * 32:(d + 1) * 32, :]
    reduce_send(0, q1, p1)
    for c in range(2, 4):
        tokens_part(c, 1, back(r_b1, c))
    for c in range(CHUNKS):
        sent(in_sem.at[c], s_in.at[c])
    for pair in range(2):
        sent(md_sem.at[pair], s_md.at[pair])
        sent(b0_sem.at[pair], s_b0.at[pair])
        sent(b1_sem.at[pair], s_b1.at[pair])
    for n, src in enumerate((q1, q2, q3, q4, q0)):
        reduce_sent(n, src)
    reduce_take(0, p1, o1.at[1])


def finish(*refs):
    sems = refs[-1]
    copies = [pltpu.make_async_copy(refs[n], refs[n + 6], sems.at[n]) for n in range(6)]
    for copy in copies:
        copy.start()
    for copy in copies:
        copy.wait()


def shards(scale, tokens, cotangent, first, second, third, fourth):
    rows = tokens.shape[0]
    T = rows // CHUNKS
    any_spec = pl.BlockSpec(memory_space=pl.ANY)
    shape = jax.ShapeDtypeStruct
    grads = [(2, 32, 256), (2, 32, 1024), (2, 128, 256), (2, 32, 256)]
    sums = [(32, 256), (32, 256)] + grads[1:]
    outs = [(tokens.shape, BF16), (tokens.shape, BF16)] + [(s, F32) for s in grads]
    parts = pl.pallas_call(
        functools.partial(kernel, scale),
        out_shape=[pltpu.VMEM(s, d) for s, d in outs],
        in_specs=[any_spec] * 6,
        out_specs=[pl.BlockSpec(memory_space=pltpu.VMEM)] * 6,
        scratch_shapes=[
            pltpu.VMEM(tokens.shape, BF16),
            pltpu.VMEM(tokens.shape, BF16),
            pltpu.VMEM(first.shape, BF16),
            pltpu.VMEM(second.shape, BF16),
            pltpu.VMEM(third.shape, BF16),
            pltpu.VMEM(fourth.shape, BF16),
            pltpu.VMEM((2, 256, 256), BF16),
            pltpu.VMEM((2, 256, 1024), BF16),
            pltpu.VMEM((2, 1024, 256), BF16),
            pltpu.VMEM((2, 256, 1024), BF16),
            pltpu.VMEM((2, 256, 256), BF16),
            pltpu.VMEM((CHUNKS, 2, 256, T), BF16),
            pltpu.VMEM((CHUNKS, 16, 2, 32, T), BF16),
            pltpu.VMEM((CHUNKS, 16, 2, 32, T), BF16),
            pltpu.VMEM((2, 16, 2, 32, T), BF16),
            pltpu.VMEM((2, 16, 2, 32, T), BF16),
            pltpu.VMEM((2, 16, 2, 16, T), BF16),
            pltpu.VMEM((2, 16, 2, 16, T), BF16),
            pltpu.VMEM((2, 16, 2, 16, T), BF16),
            pltpu.VMEM((2, 16, 2, 16, T), BF16),
            pltpu.VMEM((1024, T), BF16),
            pltpu.VMEM((1024, T), BF16),
            pltpu.VMEM((2, 256, T), F32),
            pltpu.VMEM((2, 256, T), F32),
            pltpu.VMEM((2, 256, 256), F32),
            pltpu.VMEM((2, 1024, 256), F32),
            pltpu.VMEM((2, 1024, 256), F32),
            pltpu.VMEM((2, 256, 256), F32),
        ]
        + [pltpu.VMEM((8,) + s, BF16) for s in sums] * 2
        + [
            pltpu.SemaphoreType.DMA((4,)),
            pltpu.SemaphoreType.DMA((CHUNKS,)),
            pltpu.SemaphoreType.DMA((CHUNKS,)),
            pltpu.SemaphoreType.DMA((CHUNKS, 2)),
            pltpu.SemaphoreType.DMA((2, 2)),
            pltpu.SemaphoreType.DMA((2, 2)),
            pltpu.SemaphoreType.DMA((2, 2)),
            pltpu.SemaphoreType.DMA((5,)),
            pltpu.SemaphoreType.DMA((5,)),
        ],
        compiler_params=pltpu.CompilerParams(
            collective_id=0, has_side_effects=True, vmem_limit_bytes=48 * 1024 * 1024
        ),
        cost_estimate=pl.CostEstimate(
            flops=16 * 10**9, bytes_accessed=12 * 2**20, transcendentals=4 * 2**20
        ),
    )(*(pltpu.with_memory_space_constraint(a, pltpu.HBM) for a in (tokens, cotangent, first, second, third, fourth)))
    return pl.pallas_call(
        finish,
        out_shape=[shape(s, d) for s, d in outs],
        in_specs=[pl.BlockSpec(memory_space=pltpu.VMEM)] * 6,
        out_specs=[any_spec] * 6,
        scratch_shapes=[pltpu.SemaphoreType.DMA((6,))],
        compiler_params=pltpu.CompilerParams(vmem_limit_bytes=1024 * 1024),
    )(*parts)


def solution(mesh):
    in_specs = (P("dp", "tensor"),) * 2 + (P("tensor", None, None),) * 4
    out_specs = (P("dp", "tensor"),) * 2 + (P("tensor", "dp", None),) * 4

    def run(tokens, *rest):
        scale = tokens.shape[0] ** -0.5
        step = jax.shard_map(
            functools.partial(shards, scale), mesh=mesh, in_specs=in_specs, out_specs=out_specs, check_vma=False
        )
        return step(tokens, *rest)

    return run
```

```python
import functools
import math

import jax
import jax.numpy as jnp
from jax import lax
from jax.experimental import pallas as pl
from jax.experimental.pallas import tpu as pltpu
from jax.sharding import PartitionSpec as P

F32 = jnp.float32
BF16 = jnp.bfloat16
CHUNKS = 4
TILE = 128
FAR = ((2, 2), (2, 1), (2, 3), (1, 2), (3, 2), (0, 2), (2, 0), (1, 1), (3, 3), (1, 3), (3, 1), (1, 0), (3, 0), (0, 1), (0, 3))
ROWS = ((2, 1), (2, 0), (1, 1), (3, 1), (1, 0), (3, 0), (0, 1))
COEF = math.sqrt(2.0 / math.pi)
CUBE = 0.044715 * COEF


def dot(a, b):
    return lax.dot_general(a, b, (((1,), (0,)), ((), ())), preferred_element_type=F32)


def dot_nt(a, b):
    return lax.dot_general(a, b, (((1,), (1,)), ((), ())), preferred_element_type=F32)


def perm_in():
    i = lax.broadcasted_iota(jnp.int32, (256, 256), 0)
    j = lax.broadcasted_iota(jnp.int32, (256, 256), 1)
    return jnp.where((i & 7) * 32 + (i >> 3) == j, 1.0, 0.0).astype(BF16)


def perm_out():
    i = lax.broadcasted_iota(jnp.int32, (256, 256), 0)
    j = lax.broadcasted_iota(jnp.int32, (256, 256), 1)
    return jnp.where((i & 31) * 8 + (i >> 5) == j, 1.0, 0.0).astype(BF16)


def pack(slot, a, b):
    for q in range(16):
        lo = q * 16
        rows = [a[lo:lo + 8], b[lo:lo + 8], a[lo + 8:lo + 16], b[lo + 8:lo + 16]]
        slot(q)[...] = jnp.concatenate(rows, axis=0).astype(BF16)


def kernel(scale,
           x_hbm, g_hbm, w1_hbm, w2_hbm, w3_hbm, w4_hbm,
           lo, tg, o1, o2, o3, o4, p1,
           x, g, w1, w2, w3, w4, w1t, w2p, w2t, w3t, w4p, xt,
           s_in, r_in, s_md, r_md, s_b0, r_b0, s_b1, r_b1, hid, pgr, md, bi,
           a1, a2, a3, a4, q0, q1, q2, q3, q4, p0, p2, p3, p4,
           wsem, xsem, gsem, in_sem, md_sem, b0_sem, b1_sem, qsem, psem):
    T = x.shape[0] // CHUNKS
    dp = lax.axis_index("dp")
    me = lax.axis_index("tensor")
    mz, mx = lax.div(me, 4), lax.rem(me, 4)
    row, core = lax.div(dp, 2), lax.rem(dp, 2)
    turn = 1 - 2 * core

    def rows_of(c):
        return pl.ds(pl.multiple_of(c * T, T), T)

    loads = [
        pltpu.make_async_copy(h, v, wsem.at[i])
        for i, (h, v) in enumerate([(w1_hbm, w1), (w4_hbm, w4), (w2_hbm, w2), (w3_hbm, w3)])
    ]

    def load_x(c):
        return pltpu.make_async_copy(x_hbm.at[rows_of(c)], x.at[rows_of(c)], xsem.at[c])

    def load_g(c):
        return pltpu.make_async_copy(g_hbm.at[rows_of(c)], g.at[rows_of(c)], gsem.at[c])

    def peer(dx, dz):
        return {"tensor": lax.rem(mz + dz, 4) * 4 + lax.rem(mx + dx, 4)}

    def other(dy, dc):
        return {"dp": lax.rem(row + dy, 4) * 2 + (core + dc * turn)}

    barrier = pltpu.get_barrier_semaphore()
    for dx, dz in FAR:
        pl.semaphore_signal(barrier, inc=1, device_id=peer(dx, dz))
    for dy, dc in ROWS:
        pl.semaphore_signal(barrier, inc=1, device_id=other(dy, dc))
    loads[0].start()
    load_x(0).start()
    loads[1].start()
    load_g(0).start()
    for c in range(1, CHUNKS):
        load_x(c).start()
        load_g(c).start()
    loads[2].start()
    loads[3].start()

    def send(sems, view, src, dst):
        pltpu.make_async_copy(view(src, me), view(dst, me), sems.at[1]).start()
        for dx, dz in FAR:
            ax = (dx + core * (dz - dx)) * turn
            az = (dz + core * (dx - dz)) * turn
            q = lax.rem(mz + az + 4, 4) * 4 + lax.rem(mx + ax + 4, 4)
            pltpu.make_async_remote_copy(
                src_ref=view(src, q), dst_ref=view(dst, me),
                send_sem=sems.at[0], recv_sem=sems.at[1],
                device_id={"tensor": q},
            ).start()

    def arrive(sems, dst):
        pltpu.make_async_copy(dst, dst, sems.at[1]).wait()

    def sent(sems, src):
        part = src.at[pl.ds(0, 15)]
        pltpu.make_async_copy(part, part, sems.at[0]).wait()

    def mix_x(c):
        load_x(c).wait()
        a, b = (dot_nt(w1t[n], x[rows_of(c), n * 256:(n + 1) * 256]) for n in range(2))
        pack(lambda q: s_in.at[c, q, 0], a, b)

    def mix_g(c):
        load_g(c).wait()
        a, b = (dot_nt(w4p[n], g[rows_of(c), n * 256:(n + 1) * 256]) for n in range(2))
        pack(lambda q: s_in.at[c, q, 1], a, b)

    loads[0].wait()
    for b in range(2):
        w1t[b] = w1[b].T
    mix_x(0)
    pl.semaphore_wait(barrier, 22)
    send(in_sem.at[0], lambda ref, q: ref.at[0, q, 0], s_in, r_in)
    loads[1].wait()
    pin = perm_in()
    for b in range(2):
        w4p[b] = dot(pin, w4[b]).astype(BF16)
    mix_g(0)
    send(in_sem.at[0], lambda ref, q: ref.at[0, q, 1], s_in, r_in)

    def mix(c, carry):
        mix_x(c)
        mix_g(c)
        send(in_sem.at[c], lambda ref, q: ref.at[c, q], s_in, r_in)
        return carry

    lax.fori_loop(1, CHUNKS, mix, 0)

    loads[2].wait()
    loads[3].wait()
    for b in range(2):
        w2p[b] = dot(pin, w2[b]).astype(BF16)
        w2t[b] = w2p[b].T
        w3t[b] = w3[b].T
    a1[...] = jnp.zeros_like(a1)
    a2[...] = jnp.zeros_like(a2)
    a3[...] = jnp.zeros_like(a3)
    a4[...] = jnp.zeros_like(a4)

    def hidden_stage(c, pair):
        arrive(in_sem.at[c], r_in.at[c])
        for k in range(2):
            arr = r_in[c, :, 0, k * 16:(k + 1) * 16, :].reshape(256, T)
            bd = r_in[c, :, 1, k * 16:(k + 1) * 16, :].reshape(256, T)

            def tile(n, inner):
                o = pl.ds(pl.multiple_of(n * TILE, TILE), TILE)
                v = dot(w2t[k, o, :], arr)
                hg = dot(w3[k, o, :], bd)
                v2 = v * v
                t = jnp.tanh(v * (COEF + CUBE * v2))
                h = 0.5 + 0.5 * t
                hid[o, :] = (v * h).astype(BF16)
                slope = h + (0.5 * v) * (1.0 - t * t) * (COEF + (3.0 * CUBE) * v2)
                pgr[o, :] = (slope * hg).astype(BF16)
                return inner

            lax.fori_loop(0, 1024 // TILE, tile, 0)
            md[k] = dot(w3t[k], hid[...])
            bi[k] = dot(w2p[k], pgr[...])
            a3[k] += dot_nt(hid[...], bd)
            a2[k] += dot_nt(pgr[...], arr)
        half = c % 2
        pack(lambda q: s_md.at[pair, q, half], md[0], md[1])

        for q in range(16):
            for n, dst in enumerate((s_b0, s_b1)):
                low = q * 16 + n * 8
                rows = [bi[0, low:low + 8], bi[1, low:low + 8]]
                dst[pair, q, half] = jnp.concatenate(rows, axis=0).astype(BF16)
        return pair

    def hidden_pair(pair, carry):
        lax.fori_loop(2 * pair, 2 * pair + 2, hidden_stage, pair)
        send(md_sem.at[pair], lambda ref, q: ref.at[pair, q], s_md, r_md)
        send(b0_sem.at[pair], lambda ref, q: ref.at[pair, q], s_b0, r_b0)
        return carry

    lax.fori_loop(0, 2, hidden_pair, 0)
    for pair in range(2):
        send(b1_sem.at[pair], lambda ref, q: ref.at[pair, q], s_b1, r_b1)

    def reduce_send(n, src, dst):
        for dy, dc in ROWS:
            p = other(dy, dc)
            pltpu.make_async_remote_copy(
                src_ref=src.at[p["dp"]], dst_ref=dst.at[dp],
                send_sem=qsem.at[n], recv_sem=psem.at[n],
                device_id=p,
            ).start()
        pltpu.make_async_copy(src.at[dp], dst.at[dp], psem.at[n]).start()

    def reduce_sent(n, src):
        part = src.at[pl.ds(0, 7)]
        pltpu.make_async_copy(part, part, qsem.at[n]).wait()

    def reduce_take(n, dst, out):
        pltpu.make_async_copy(dst, dst, psem.at[n]).wait()
        total = dst[0].astype(F32)
        for p in range(1, 8):
            total += dst[p].astype(F32)
        out[...] = total

    pout = perm_out()
    for k in range(2):
        for d in range(8):
            q3[d, k] = (a3[k, d * 128:(d + 1) * 128, :] * scale).astype(BF16)
    reduce_send(2, q3, p3)
    for k in range(2):
        full = dot_nt(pout, (a2[k] * scale).astype(BF16)).astype(BF16)
        for d in range(8):
            q2[d, k] = full[d * 32:(d + 1) * 32, :]
    reduce_send(1, q2, p2)

    def turn_x(c, carry):
        for n in range(2):
            xt[c, n] = x[rows_of(c), n * 256:(n + 1) * 256].T
        return carry

    lax.fori_loop(0, CHUNKS, turn_x, 0)

    def out_stage(c, pair):
        rows = rows_of(c)
        for n in range(2):
            cols = slice(n * 256, (n + 1) * 256)
            ret = r_md[pair, :, c % 2, n * 16:(n + 1) * 16, :].reshape(256, T)
            a4[n] += dot(ret, g[rows, cols])
            lo[rows, cols] = dot(ret.T, w4p[n]).astype(BF16)
        return pair

    def first_part(c, n, ret):
        a1[n] += dot_nt(xt[c, n], ret)

    def tokens_part(c, n, ret):
        tg[rows_of(c), n * 256:(n + 1) * 256] = dot(ret.T, w1t[n]).astype(BF16)

    def back(r_b, c):
        return r_b[c // 2, :, c % 2].reshape(256, T)

    def in_stage(c, carry):
        ret = back(r_b0, c)
        first_part(c, 0, ret)
        tokens_part(c, 0, ret)
        return carry

    arrive(md_sem.at[0], r_md.at[0])
    lax.fori_loop(0, 2, out_stage, 0)
    arrive(b0_sem.at[0], r_b0.at[0])
    lax.fori_loop(0, 2, in_stage, 0)
    reduce_take(2, p3, o3)
    reduce_take(1, p2, o2)
    arrive(md_sem.at[1], r_md.at[1])
    lax.fori_loop(2, 4, out_stage, 1)
    for n in range(2):
        full = dot(pout, (a4[n] * scale).astype(BF16)).astype(BF16)
        for d in range(8):
            q4[d, n] = full[d * 32:(d + 1) * 32, :]
    reduce_send(3, q4, p4)
    arrive(b0_sem.at[1], r_b0.at[1])
    lax.fori_loop(2, 4, in_stage, 0)
    full = (a1[0] * scale).astype(BF16)
    for d in range(8):
        q0[d] = full[d * 32:(d + 1) * 32, :]
    reduce_send(4, q0, p0)
    arrive(b1_sem.at[0], r_b1.at[0])
    for c in range(2):
        first_part(c, 1, back(r_b1, c))
        tokens_part(c, 1, back(r_b1, c))
    reduce_take(3, p4, o4)
    reduce_take(4, p0, o1)
    for c in range(CHUNKS):
        sent(in_sem.at[c], s_in.at[c])
    for pair in range(2):
        sent(md_sem.at[pair], s_md.at[pair])
        sent(b0_sem.at[pair], s_b0.at[pair])
    sent(b1_sem.at[0], s_b1.at[0])
    for n, src in ((1, q2), (2, q3), (3, q4), (4, q0)):
        reduce_sent(n, src)
    arrive(b1_sem.at[1], r_b1.at[1])
    full = a1[1] + dot_nt(xt[2, 1], back(r_b1, 2)) + dot_nt(xt[3, 1], back(r_b1, 3))
    full = (full * scale).astype(BF16)
    for d in range(8):
        q1[d] = full[d * 32:(d + 1) * 32, :]
    reduce_send(0, q1, p1)
    for c in range(2, 4):
        tokens_part(c, 1, back(r_b1, c))
    sent(b1_sem.at[1], s_b1.at[1])
    reduce_sent(0, q1)
    pltpu.make_async_copy(p1, p1, psem.at[0]).wait()


def finish(lo, tg, o1, o2, o3, o4, p1, lo_hbm, tg_hbm, g1, g2, g3, g4, last, sems):
    pairs = [(lo, lo_hbm), (tg, tg_hbm), (o2, g2), (o3, g3), (o4, g4), (o1, g1.at[0]), (last, g1.at[1])]
    copies = [pltpu.make_async_copy(src, dst, sems.at[n]) for n, (src, dst) in enumerate(pairs)]
    for copy in copies[:-1]:
        copy.start()
    total = p1[0].astype(F32)
    for p in range(1, 8):
        total += p1[p].astype(F32)
    last[...] = total
    copies[-1].start()
    for copy in copies:
        copy.wait()


def shards(scale, tokens, cotangent, first, second, third, fourth):
    rows = tokens.shape[0]
    T = rows // CHUNKS
    any_spec = pl.BlockSpec(memory_space=pl.ANY)
    shape = jax.ShapeDtypeStruct
    grads = [(2, 32, 256), (2, 32, 1024), (2, 128, 256), (2, 32, 256)]
    sums = [(32, 256), (32, 256)] + grads[1:]
    outs = [(tokens.shape, BF16), (tokens.shape, BF16)] + [(s, F32) for s in grads]
    kept = outs[:2] + [((32, 256), F32)] + outs[3:] + [((8, 32, 256), BF16)]
    parts = pl.pallas_call(
        functools.partial(kernel, scale),
        out_shape=[pltpu.VMEM(s, d) for s, d in kept],
        in_specs=[any_spec] * 6,
        out_specs=[pl.BlockSpec(memory_space=pltpu.VMEM)] * 7,
        scratch_shapes=[
            pltpu.VMEM(tokens.shape, BF16),
            pltpu.VMEM(tokens.shape, BF16),
            pltpu.VMEM(first.shape, BF16),
            pltpu.VMEM(second.shape, BF16),
            pltpu.VMEM(third.shape, BF16),
            pltpu.VMEM(fourth.shape, BF16),
            pltpu.VMEM((2, 256, 256), BF16),
            pltpu.VMEM((2, 256, 1024), BF16),
            pltpu.VMEM((2, 1024, 256), BF16),
            pltpu.VMEM((2, 256, 1024), BF16),
            pltpu.VMEM((2, 256, 256), BF16),
            pltpu.VMEM((CHUNKS, 2, 256, T), BF16),
            pltpu.VMEM((CHUNKS, 16, 2, 32, T), BF16),
            pltpu.VMEM((CHUNKS, 16, 2, 32, T), BF16),
            pltpu.VMEM((2, 16, 2, 32, T), BF16),
            pltpu.VMEM((2, 16, 2, 32, T), BF16),
            pltpu.VMEM((2, 16, 2, 16, T), BF16),
            pltpu.VMEM((2, 16, 2, 16, T), BF16),
            pltpu.VMEM((2, 16, 2, 16, T), BF16),
            pltpu.VMEM((2, 16, 2, 16, T), BF16),
            pltpu.VMEM((1024, T), BF16),
            pltpu.VMEM((1024, T), BF16),
            pltpu.VMEM((2, 256, T), F32),
            pltpu.VMEM((2, 256, T), F32),
            pltpu.VMEM((2, 256, 256), F32),
            pltpu.VMEM((2, 1024, 256), F32),
            pltpu.VMEM((2, 1024, 256), F32),
            pltpu.VMEM((2, 256, 256), F32),
        ]
        + [pltpu.VMEM((8,) + s, BF16) for s in sums + sums[:1] + sums[2:]]
        + [
            pltpu.SemaphoreType.DMA((4,)),
            pltpu.SemaphoreType.DMA((CHUNKS,)),
            pltpu.SemaphoreType.DMA((CHUNKS,)),
            pltpu.SemaphoreType.DMA((CHUNKS, 2)),
            pltpu.SemaphoreType.DMA((2, 2)),
            pltpu.SemaphoreType.DMA((2, 2)),
            pltpu.SemaphoreType.DMA((2, 2)),
            pltpu.SemaphoreType.DMA((5,)),
            pltpu.SemaphoreType.DMA((5,)),
        ],
        compiler_params=pltpu.CompilerParams(
            collective_id=0, has_side_effects=True, vmem_limit_bytes=48 * 1024 * 1024
        ),
        cost_estimate=pl.CostEstimate(
            flops=16 * 10**9, bytes_accessed=12 * 2**20, transcendentals=4 * 2**20
        ),
    )(*(pltpu.with_memory_space_constraint(a, pltpu.HBM) for a in (tokens, cotangent, first, second, third, fourth)))
    return pl.pallas_call(
        finish,
        out_shape=[shape(s, d) for s, d in outs],
        in_specs=[pl.BlockSpec(memory_space=pltpu.VMEM)] * 7,
        out_specs=[any_spec] * 6,
        scratch_shapes=[pltpu.VMEM((32, 256), F32), pltpu.SemaphoreType.DMA((7,))],
        compiler_params=pltpu.CompilerParams(vmem_limit_bytes=1024 * 1024),
    )(*parts)


def solution(mesh):
    in_specs = (P("dp", "tensor"),) * 2 + (P("tensor", None, None),) * 4
    out_specs = (P("dp", "tensor"),) * 2 + (P("tensor", "dp", None),) * 4

    def run(tokens, *rest):
        scale = tokens.shape[0] ** -0.5
        step = jax.shard_map(
            functools.partial(shards, scale), mesh=mesh, in_specs=in_specs, out_specs=out_specs, check_vma=False
        )
        return step(tokens, *rest)

    return run
```

```python
import functools
import math

import jax
import jax.numpy as jnp
from jax import lax
from jax.experimental import pallas as pl
from jax.experimental.pallas import tpu as pltpu
from jax.sharding import PartitionSpec as P

F32 = jnp.float32
BF16 = jnp.bfloat16
CHUNKS = 4
TILE = 128
FAR = ((2, 2), (2, 1), (2, 3), (1, 2), (3, 2), (0, 2), (2, 0), (1, 1), (3, 3), (1, 3), (3, 1), (1, 0), (3, 0), (0, 1), (0, 3))
ROWS = ((2, 1), (2, 0), (1, 1), (3, 1), (1, 0), (3, 0), (0, 1))
COEF = math.sqrt(2.0 / math.pi)
CUBE = 0.044715 * COEF


def dot(a, b):
    return lax.dot_general(a, b, (((1,), (0,)), ((), ())), preferred_element_type=F32)


def dot_nt(a, b):
    return lax.dot_general(a, b, (((1,), (1,)), ((), ())), preferred_element_type=F32)


def perm_in():
    i = lax.broadcasted_iota(jnp.int32, (256, 256), 0)
    j = lax.broadcasted_iota(jnp.int32, (256, 256), 1)
    return jnp.where((i & 7) * 32 + (i >> 3) == j, 1.0, 0.0).astype(BF16)


def perm_out():
    i = lax.broadcasted_iota(jnp.int32, (256, 256), 0)
    j = lax.broadcasted_iota(jnp.int32, (256, 256), 1)
    return jnp.where((i & 31) * 8 + (i >> 5) == j, 1.0, 0.0).astype(BF16)


def pack(slot, a, b):
    for q in range(16):
        lo = q * 16
        rows = [a[lo:lo + 8], b[lo:lo + 8], a[lo + 8:lo + 16], b[lo + 8:lo + 16]]
        slot(q)[...] = jnp.concatenate(rows, axis=0).astype(BF16)


def kernel(scale,
           x_hbm, g_hbm, w1_hbm, w2_hbm, w3_hbm, w4_hbm,
           lo, tg, o1, o2, o3, o4,
           x, g, w1, w2, w3, w4, w1t, w2p, w2t, w3t, w4p, xt,
           s_in, r_in, s_md, r_md, s_b0, r_b0, s_b1, r_b1, hid, pgr, md, bi,
           a1, a2, a3, a4, q0, q1, q2, q3, q4, p0, p1, p2, p3, p4,
           wsem, xsem, gsem, in_sem, md_sem, b0_sem, b1_sem, qsem, psem):
    T = x.shape[0] // CHUNKS
    dp = lax.axis_index("dp")
    me = lax.axis_index("tensor")
    mz, mx = me // 4, me % 4
    core = dp % 2
    turn = 1 - 2 * core

    def rows_of(c):
        return pl.ds(pl.multiple_of(c * T, T), T)

    loads = [
        pltpu.make_async_copy(h, v, wsem.at[i])
        for i, (h, v) in enumerate([(w1_hbm, w1), (w4_hbm, w4), (w2_hbm, w2), (w3_hbm, w3)])
    ]

    def load_x(c):
        return pltpu.make_async_copy(x_hbm.at[rows_of(c)], x.at[rows_of(c)], xsem.at[c])

    def load_g(c):
        return pltpu.make_async_copy(g_hbm.at[rows_of(c)], g.at[rows_of(c)], gsem.at[c])

    def peer(dx, dz):
        return {"tensor": ((mz + dz) % 4) * 4 + (mx + dx) % 4}

    def other(dy, dc):
        return {"dp": ((dp // 2 + dy) % 4) * 2 + (core + dc) % 2}

    barrier = pltpu.get_barrier_semaphore()
    for dx, dz in FAR:
        pl.semaphore_signal(barrier, inc=1, device_id=peer(dx, dz))
    for dy, dc in ROWS:
        pl.semaphore_signal(barrier, inc=1, device_id=other(dy, dc))
    loads[0].start()
    load_x(0).start()
    loads[1].start()
    load_g(0).start()
    for c in range(1, CHUNKS):
        load_x(c).start()
        load_g(c).start()
    loads[2].start()
    loads[3].start()

    def send(sems, view, src, dst, order=FAR):
        if FAR[0] in order:
            pltpu.make_async_copy(view(src, me), view(dst, me), sems.at[1]).start()
        for dx, dz in order:
            ax = (dx + core * (dz - dx)) * turn
            az = (dz + core * (dx - dz)) * turn
            q = ((mz + az + 4) % 4) * 4 + (mx + ax + 4) % 4
            pltpu.make_async_remote_copy(
                src_ref=view(src, q), dst_ref=view(dst, me),
                send_sem=sems.at[0], recv_sem=sems.at[1],
                device_id={"tensor": q},
            ).start()

    def arrive(sems, dst):
        pltpu.make_async_copy(dst, dst, sems.at[1]).wait()

    def sent(sems, src):
        part = src.at[pl.ds(0, 15)]
        pltpu.make_async_copy(part, part, sems.at[0]).wait()

    def mix_x(c):
        load_x(c).wait()
        a, b = (dot_nt(w1t[n], x[rows_of(c), n * 256:(n + 1) * 256]) for n in range(2))
        pack(lambda q: s_in.at[c, q, 0], a, b)

    def mix_g(c):
        load_g(c).wait()
        a, b = (dot_nt(w4p[n], g[rows_of(c), n * 256:(n + 1) * 256]) for n in range(2))
        pack(lambda q: s_in.at[c, q, 1], a, b)

    loads[0].wait()
    for b in range(2):
        w1t[b] = w1[b].T
    mix_x(0)
    pl.semaphore_wait(barrier, 22)
    send(in_sem.at[0], lambda ref, q: ref.at[0, q, 0], s_in, r_in)
    loads[1].wait()
    pin = perm_in()
    for b in range(2):
        w4p[b] = dot(pin, w4[b]).astype(BF16)
    mix_g(0)
    send(in_sem.at[0], lambda ref, q: ref.at[0, q, 1], s_in, r_in)

    def mix(c, carry):
        mix_x(c)
        mix_g(c)
        send(in_sem.at[c], lambda ref, q: ref.at[c, q], s_in, r_in)
        return carry

    lax.fori_loop(1, CHUNKS, mix, 0)

    loads[2].wait()
    loads[3].wait()
    for b in range(2):
        w2p[b] = dot(pin, w2[b]).astype(BF16)
        w2t[b] = w2p[b].T
        w3t[b] = w3[b].T
    a1[...] = jnp.zeros_like(a1)
    a2[...] = jnp.zeros_like(a2)
    a3[...] = jnp.zeros_like(a3)
    a4[...] = jnp.zeros_like(a4)

    def hidden_stage(c, pair):
        arrive(in_sem.at[c], r_in.at[c])
        for k in range(2):
            arr = r_in[c, :, 0, k * 16:(k + 1) * 16, :].reshape(256, T)
            bd = r_in[c, :, 1, k * 16:(k + 1) * 16, :].reshape(256, T)

            def tile(n, inner):
                o = pl.ds(pl.multiple_of(n * TILE, TILE), TILE)
                v = dot(w2t[k, o, :], arr)
                hg = dot(w3[k, o, :], bd)
                v2 = v * v
                t = jnp.tanh(v * (COEF + CUBE * v2))
                h = 0.5 + 0.5 * t
                hid[o, :] = (v * h).astype(BF16)
                slope = h + (0.5 * v) * (1.0 - t * t) * (COEF + (3.0 * CUBE) * v2)
                pgr[o, :] = (slope * hg).astype(BF16)
                return inner

            lax.fori_loop(0, 1024 // TILE, tile, 0)
            md[k] = dot(w3t[k], hid[...])
            bi[k] = dot(w2p[k], pgr[...])
            a3[k] += dot_nt(hid[...], bd)
            a2[k] += dot_nt(pgr[...], arr)
        half = c % 2
        pack(lambda q: s_md.at[pair, q, half], md[0], md[1])

        for q in range(16):
            for n, dst in enumerate((s_b0, s_b1)):
                low = q * 16 + n * 8
                rows = [bi[0, low:low + 8], bi[1, low:low + 8]]
                dst[pair, q, half] = jnp.concatenate(rows, axis=0).astype(BF16)
        return pair

    def hidden_pair(pair, carry):
        lax.fori_loop(2 * pair, 2 * pair + 2, hidden_stage, pair)
        send(md_sem.at[pair], lambda ref, q: ref.at[pair, q], s_md, r_md)
        send(b0_sem.at[pair], lambda ref, q: ref.at[pair, q], s_b0, r_b0)
        return carry

    lax.fori_loop(0, 2, hidden_pair, 0)
    for order in (FAR[:5], FAR[5:11], FAR[11:]):
        for pair in range(2):
            send(b1_sem.at[pair], lambda ref, q: ref.at[pair, q], s_b1, r_b1, order)

    def reduce_send(n, src, dst):
        for dy, dc in ROWS:
            p = other(dy, dc)
            pltpu.make_async_remote_copy(
                src_ref=src.at[p["dp"]], dst_ref=dst.at[dp],
                send_sem=qsem.at[n], recv_sem=psem.at[n],
                device_id=p,
            ).start()
        pltpu.make_async_copy(src.at[dp], dst.at[dp], psem.at[n]).start()

    def reduce_sent(n, src):
        part = src.at[pl.ds(0, 7)]
        pltpu.make_async_copy(part, part, qsem.at[n]).wait()

    def reduce_take(n, dst, out):
        pltpu.make_async_copy(dst, dst, psem.at[n]).wait()
        total = dst[0].astype(F32)
        for p in range(1, 8):
            total += dst[p].astype(F32)
        out[...] = total

    pout = perm_out()
    for k in range(2):
        for d in range(8):
            q3[d, k] = (a3[k, d * 128:(d + 1) * 128, :] * scale).astype(BF16)
    reduce_send(2, q3, p3)
    for k in range(2):
        full = dot_nt(pout, (a2[k] * scale).astype(BF16)).astype(BF16)
        for d in range(8):
            q2[d, k] = full[d * 32:(d + 1) * 32, :]
    reduce_send(1, q2, p2)

    def turn_x(c, carry):
        for n in range(2):
            xt[c, n] = x[rows_of(c), n * 256:(n + 1) * 256].T
        return carry

    lax.fori_loop(0, CHUNKS, turn_x, 0)

    def out_stage(c, pair):
        rows = rows_of(c)
        for n in range(2):
            cols = slice(n * 256, (n + 1) * 256)
            ret = r_md[pair, :, c % 2, n * 16:(n + 1) * 16, :].reshape(256, T)
            a4[n] += dot(ret, g[rows, cols])
            lo[rows, cols] = dot(ret.T, w4p[n]).astype(BF16)
        return pair

    def first_part(c, n, ret):
        a1[n] += dot_nt(xt[c, n], ret)

    def tokens_part(c, n, ret):
        tg[rows_of(c), n * 256:(n + 1) * 256] = dot(ret.T, w1t[n]).astype(BF16)

    def back(r_b, c):
        return r_b[c // 2, :, c % 2].reshape(256, T)

    def in_stage(c, carry):
        ret = back(r_b0, c)
        first_part(c, 0, ret)
        tokens_part(c, 0, ret)
        return carry

    arrive(md_sem.at[0], r_md.at[0])
    lax.fori_loop(0, 2, out_stage, 0)
    arrive(b0_sem.at[0], r_b0.at[0])
    lax.fori_loop(0, 2, in_stage, 0)
    reduce_take(2, p3, o3)
    reduce_take(1, p2, o2)
    arrive(md_sem.at[1], r_md.at[1])
    lax.fori_loop(2, 4, out_stage, 1)
    for n in range(2):
        full = dot(pout, (a4[n] * scale).astype(BF16)).astype(BF16)
        for d in range(8):
            q4[d, n] = full[d * 32:(d + 1) * 32, :]
    reduce_send(3, q4, p4)
    arrive(b0_sem.at[1], r_b0.at[1])
    lax.fori_loop(2, 4, in_stage, 0)
    full = (a1[0] * scale).astype(BF16)
    for d in range(8):
        q0[d] = full[d * 32:(d + 1) * 32, :]
    reduce_send(4, q0, p0)
    arrive(b1_sem.at[0], r_b1.at[0])
    for c in range(2):
        first_part(c, 1, back(r_b1, c))
        tokens_part(c, 1, back(r_b1, c))
    reduce_take(3, p4, o4)
    reduce_take(4, p0, o1.at[0])
    arrive(b1_sem.at[1], r_b1.at[1])
    full = a1[1] + dot_nt(xt[2, 1], back(r_b1, 2)) + dot_nt(xt[3, 1], back(r_b1, 3))
    full = (full * scale).astype(BF16)
    for d in range(8):
        q1[d] = full[d * 32:(d + 1) * 32, :]
    reduce_send(0, q1, p1)
    for c in range(2, 4):
        tokens_part(c, 1, back(r_b1, c))
    for c in range(CHUNKS):
        sent(in_sem.at[c], s_in.at[c])
    for pair in range(2):
        sent(md_sem.at[pair], s_md.at[pair])
        sent(b0_sem.at[pair], s_b0.at[pair])
        sent(b1_sem.at[pair], s_b1.at[pair])
    for n, src in enumerate((q1, q2, q3, q4, q0)):
        reduce_sent(n, src)
    reduce_take(0, p1, o1.at[1])


def finish(*refs):
    sems = refs[-1]
    copies = [pltpu.make_async_copy(refs[n], refs[n + 6], sems.at[n]) for n in range(6)]
    for copy in copies:
        copy.start()
    for copy in copies:
        copy.wait()


def shards(scale, tokens, cotangent, first, second, third, fourth):
    rows = tokens.shape[0]
    T = rows // CHUNKS
    any_spec = pl.BlockSpec(memory_space=pl.ANY)
    shape = jax.ShapeDtypeStruct
    grads = [(2, 32, 256), (2, 32, 1024), (2, 128, 256), (2, 32, 256)]
    sums = [(32, 256), (32, 256)] + grads[1:]
    outs = [(tokens.shape, BF16), (tokens.shape, BF16)] + [(s, F32) for s in grads]
    parts = pl.pallas_call(
        functools.partial(kernel, scale),
        out_shape=[pltpu.VMEM(s, d) for s, d in outs],
        in_specs=[any_spec] * 6,
        out_specs=[pl.BlockSpec(memory_space=pltpu.VMEM)] * 6,
        scratch_shapes=[
            pltpu.VMEM(tokens.shape, BF16),
            pltpu.VMEM(tokens.shape, BF16),
            pltpu.VMEM(first.shape, BF16),
            pltpu.VMEM(second.shape, BF16),
            pltpu.VMEM(third.shape, BF16),
            pltpu.VMEM(fourth.shape, BF16),
            pltpu.VMEM((2, 256, 256), BF16),
            pltpu.VMEM((2, 256, 1024), BF16),
            pltpu.VMEM((2, 1024, 256), BF16),
            pltpu.VMEM((2, 256, 1024), BF16),
            pltpu.VMEM((2, 256, 256), BF16),
            pltpu.VMEM((CHUNKS, 2, 256, T), BF16),
            pltpu.VMEM((CHUNKS, 16, 2, 32, T), BF16),
            pltpu.VMEM((CHUNKS, 16, 2, 32, T), BF16),
            pltpu.VMEM((2, 16, 2, 32, T), BF16),
            pltpu.VMEM((2, 16, 2, 32, T), BF16),
            pltpu.VMEM((2, 16, 2, 16, T), BF16),
            pltpu.VMEM((2, 16, 2, 16, T), BF16),
            pltpu.VMEM((2, 16, 2, 16, T), BF16),
            pltpu.VMEM((2, 16, 2, 16, T), BF16),
            pltpu.VMEM((1024, T), BF16),
            pltpu.VMEM((1024, T), BF16),
            pltpu.VMEM((2, 256, T), F32),
            pltpu.VMEM((2, 256, T), F32),
            pltpu.VMEM((2, 256, 256), F32),
            pltpu.VMEM((2, 1024, 256), F32),
            pltpu.VMEM((2, 1024, 256), F32),
            pltpu.VMEM((2, 256, 256), F32),
        ]
        + [pltpu.VMEM((8,) + s, BF16) for s in sums] * 2
        + [
            pltpu.SemaphoreType.DMA((4,)),
            pltpu.SemaphoreType.DMA((CHUNKS,)),
            pltpu.SemaphoreType.DMA((CHUNKS,)),
            pltpu.SemaphoreType.DMA((CHUNKS, 2)),
            pltpu.SemaphoreType.DMA((2, 2)),
            pltpu.SemaphoreType.DMA((2, 2)),
            pltpu.SemaphoreType.DMA((2, 2)),
            pltpu.SemaphoreType.DMA((5,)),
            pltpu.SemaphoreType.DMA((5,)),
        ],
        compiler_params=pltpu.CompilerParams(
            collective_id=0, has_side_effects=True, vmem_limit_bytes=48 * 1024 * 1024
        ),
        cost_estimate=pl.CostEstimate(
            flops=16 * 10**9, bytes_accessed=12 * 2**20, transcendentals=4 * 2**20
        ),
    )(*(pltpu.with_memory_space_constraint(a, pltpu.HBM) for a in (tokens, cotangent, first, second, third, fourth)))
    return pl.pallas_call(
        finish,
        out_shape=[shape(s, d) for s, d in outs],
        in_specs=[pl.BlockSpec(memory_space=pltpu.VMEM)] * 6,
        out_specs=[any_spec] * 6,
        scratch_shapes=[pltpu.SemaphoreType.DMA((6,))],
        compiler_params=pltpu.CompilerParams(vmem_limit_bytes=1024 * 1024),
    )(*parts)


def solution(mesh):
    in_specs = (P("dp", "tensor"),) * 2 + (P("tensor", None, None),) * 4
    out_specs = (P("dp", "tensor"),) * 2 + (P("tensor", "dp", None),) * 4

    def run(tokens, *rest):
        scale = tokens.shape[0] ** -0.5
        step = jax.shard_map(
            functools.partial(shards, scale), mesh=mesh, in_specs=in_specs, out_specs=out_specs, check_vma=False
        )
        return step(tokens, *rest)

    return run
```

```python
import functools
import math

import jax
import jax.numpy as jnp
from jax import lax
from jax.experimental import pallas as pl
from jax.experimental.pallas import tpu as pltpu
from jax.sharding import PartitionSpec as P

F32 = jnp.float32
BF16 = jnp.bfloat16
CHUNKS = 4
TILE = 128
FAR = ((2, 2), (2, 1), (2, 3), (1, 2), (3, 2), (0, 2), (2, 0), (1, 1), (3, 3), (1, 3), (3, 1), (1, 0), (3, 0), (0, 1), (0, 3))
ROWS = ((2, 1), (2, 0), (1, 1), (3, 1), (1, 0), (3, 0), (0, 1))
COEF = math.sqrt(2.0 / math.pi)
CUBE = 0.044715 * COEF


def dot(a, b):
    return lax.dot_general(a, b, (((1,), (0,)), ((), ())), preferred_element_type=F32)


def dot_nt(a, b):
    return lax.dot_general(a, b, (((1,), (1,)), ((), ())), preferred_element_type=F32)


def perm_in():
    i = lax.broadcasted_iota(jnp.int32, (256, 256), 0)
    j = lax.broadcasted_iota(jnp.int32, (256, 256), 1)
    return jnp.where((i & 7) * 32 + (i >> 3) == j, 1.0, 0.0).astype(BF16)


def perm_out():
    i = lax.broadcasted_iota(jnp.int32, (256, 256), 0)
    j = lax.broadcasted_iota(jnp.int32, (256, 256), 1)
    return jnp.where((i & 31) * 8 + (i >> 5) == j, 1.0, 0.0).astype(BF16)


def pack(slot, a, b):
    for q in range(16):
        lo = q * 16
        rows = [a[lo:lo + 8], b[lo:lo + 8], a[lo + 8:lo + 16], b[lo + 8:lo + 16]]
        slot(q)[...] = jnp.concatenate(rows, axis=0).astype(BF16)


def kernel(scale,
           x_hbm, g_hbm, w1_hbm, w2_hbm, w3_hbm, w4_hbm,
           lo, tg, o1, o2, o3, o4,
           x, g, w1, w2, w3, w4, w1t, w2p, w2t, w3t, w4p, xt,
           s_in, r_in, s_md, r_md, s_b0, r_b0, s_b1, r_b1, hid, pgr, md, bi,
           a1, a2, a3, a4, q0, q1, q2, q3, q4, p0, p1, p2, p3, p4,
           wsem, xsem, gsem, in_sem, md_sem, b0_sem, b1_sem, qsem, psem):
    T = x.shape[0] // CHUNKS
    dp = lax.axis_index("dp")
    me = lax.axis_index("tensor")
    mz, mx = lax.div(me, 4), lax.rem(me, 4)
    row, core = lax.div(dp, 2), lax.rem(dp, 2)
    turn = 1 - 2 * core

    def rows_of(c):
        return pl.ds(pl.multiple_of(c * T, T), T)

    loads = [
        pltpu.make_async_copy(h, v, wsem.at[i])
        for i, (h, v) in enumerate([(w1_hbm, w1), (w4_hbm, w4), (w2_hbm, w2), (w3_hbm, w3)])
    ]

    def load_x(c):
        return pltpu.make_async_copy(x_hbm.at[rows_of(c)], x.at[rows_of(c)], xsem.at[c])

    def load_g(c):
        return pltpu.make_async_copy(g_hbm.at[rows_of(c)], g.at[rows_of(c)], gsem.at[c])

    def peer(dx, dz):
        return {"tensor": lax.rem(mz + dz, 4) * 4 + lax.rem(mx + dx, 4)}

    def other(dy, dc):
        return {"dp": lax.rem(row + dy, 4) * 2 + (core + dc * turn)}

    barrier = pltpu.get_barrier_semaphore()
    for dx, dz in FAR:
        pl.semaphore_signal(barrier, inc=1, device_id=peer(dx, dz))
    for dy, dc in ROWS:
        pl.semaphore_signal(barrier, inc=1, device_id=other(dy, dc))
    loads[0].start()
    load_x(0).start()
    loads[1].start()
    load_g(0).start()
    for c in range(1, CHUNKS):
        load_x(c).start()
        load_g(c).start()
    loads[2].start()
    loads[3].start()

    def send(sems, view, src, dst):
        pltpu.make_async_copy(view(src, me), view(dst, me), sems.at[1]).start()
        for dx, dz in FAR:
            ax = (dx + core * (dz - dx)) * turn
            az = (dz + core * (dx - dz)) * turn
            q = lax.rem(mz + az + 4, 4) * 4 + lax.rem(mx + ax + 4, 4)
            pltpu.make_async_remote_copy(
                src_ref=view(src, q), dst_ref=view(dst, me),
                send_sem=sems.at[0], recv_sem=sems.at[1],
                device_id={"tensor": q},
            ).start()

    def arrive(sems, dst):
        pltpu.make_async_copy(dst, dst, sems.at[1]).wait()

    def sent(sems, src):
        part = src.at[pl.ds(0, 15)]
        pltpu.make_async_copy(part, part, sems.at[0]).wait()

    def mix_x(c):
        load_x(c).wait()
        a, b = (dot_nt(w1t[n], x[rows_of(c), n * 256:(n + 1) * 256]) for n in range(2))
        pack(lambda q: s_in.at[c, q, 0], a, b)

    def mix_g(c):
        load_g(c).wait()
        a, b = (dot_nt(w4p[n], g[rows_of(c), n * 256:(n + 1) * 256]) for n in range(2))
        pack(lambda q: s_in.at[c, q, 1], a, b)

    loads[0].wait()
    for b in range(2):
        w1t[b] = w1[b].T
    mix_x(0)
    pl.semaphore_wait(barrier, 22)
    send(in_sem.at[0], lambda ref, q: ref.at[0, q, 0], s_in, r_in)
    loads[1].wait()
    pin = perm_in()
    for b in range(2):
        w4p[b] = dot(pin, w4[b]).astype(BF16)
    mix_g(0)
    send(in_sem.at[0], lambda ref, q: ref.at[0, q, 1], s_in, r_in)

    def mix(c, carry):
        mix_x(c)
        mix_g(c)
        send(in_sem.at[c], lambda ref, q: ref.at[c, q], s_in, r_in)
        return carry

    lax.fori_loop(1, CHUNKS, mix, 0)

    loads[2].wait()
    loads[3].wait()
    for b in range(2):
        w2p[b] = dot(pin, w2[b]).astype(BF16)
        w2t[b] = w2p[b].T
        w3t[b] = w3[b].T
    a1[...] = jnp.zeros_like(a1)
    a2[...] = jnp.zeros_like(a2)
    a3[...] = jnp.zeros_like(a3)
    a4[...] = jnp.zeros_like(a4)

    def hidden_stage(c, pair):
        arrive(in_sem.at[c], r_in.at[c])
        for k in range(2):
            arr = r_in[c, :, 0, k * 16:(k + 1) * 16, :].reshape(256, T)
            bd = r_in[c, :, 1, k * 16:(k + 1) * 16, :].reshape(256, T)

            def tile(n, inner):
                o = pl.ds(pl.multiple_of(n * TILE, TILE), TILE)
                v = dot(w2t[k, o, :], arr)
                hg = dot(w3[k, o, :], bd)
                v2 = v * v
                t = jnp.tanh(v * (COEF + CUBE * v2))
                h = 0.5 + 0.5 * t
                hid[o, :] = (v * h).astype(BF16)
                slope = h + (0.5 * v) * (1.0 - t * t) * (COEF + (3.0 * CUBE) * v2)
                pgr[o, :] = (slope * hg).astype(BF16)
                return inner

            lax.fori_loop(0, 1024 // TILE, tile, 0)
            md[k] = dot(w3t[k], hid[...])
            bi[k] = dot(w2p[k], pgr[...])
            a3[k] += dot_nt(hid[...], bd)
            a2[k] += dot_nt(pgr[...], arr)
        half = c % 2
        pack(lambda q: s_md.at[pair, q, half], md[0], md[1])

        for q in range(16):
            for n, dst in enumerate((s_b0, s_b1)):
                low = q * 16 + n * 8
                rows = [bi[0, low:low + 8], bi[1, low:low + 8]]
                dst[pair, q, half] = jnp.concatenate(rows, axis=0).astype(BF16)
        return pair

    def hidden_pair(pair, carry):
        lax.fori_loop(2 * pair, 2 * pair + 2, hidden_stage, pair)
        send(md_sem.at[pair], lambda ref, q: ref.at[pair, q], s_md, r_md)
        send(b0_sem.at[pair], lambda ref, q: ref.at[pair, q], s_b0, r_b0)
        return carry

    lax.fori_loop(0, 2, hidden_pair, 0)
    for pair in range(2):
        send(b1_sem.at[pair], lambda ref, q: ref.at[pair, q], s_b1, r_b1)

    def reduce_send(n, src, dst):
        for dy, dc in ROWS:
            p = other(dy, dc)
            pltpu.make_async_remote_copy(
                src_ref=src.at[p["dp"]], dst_ref=dst.at[dp],
                send_sem=qsem.at[n], recv_sem=psem.at[n],
                device_id=p,
            ).start()
        pltpu.make_async_copy(src.at[dp], dst.at[dp], psem.at[n]).start()

    def reduce_sent(n, src):
        part = src.at[pl.ds(0, 7)]
        pltpu.make_async_copy(part, part, qsem.at[n]).wait()

    def reduce_take(n, dst, out):
        pltpu.make_async_copy(dst, dst, psem.at[n]).wait()
        total = dst[0].astype(F32)
        for p in range(1, 8):
            total += dst[p].astype(F32)
        out[...] = total

    pout = perm_out()
    for k in range(2):
        for d in range(8):
            q3[d, k] = (a3[k, d * 128:(d + 1) * 128, :] * scale).astype(BF16)
    reduce_send(2, q3, p3)
    for k in range(2):
        full = dot_nt(pout, (a2[k] * scale).astype(BF16)).astype(BF16)
        for d in range(8):
            q2[d, k] = full[d * 32:(d + 1) * 32, :]
    reduce_send(1, q2, p2)

    def turn_x(c, carry):
        for n in range(2):
            xt[c, n] = x[rows_of(c), n * 256:(n + 1) * 256].T
        return carry

    lax.fori_loop(0, CHUNKS, turn_x, 0)

    def out_stage(c, pair):
        rows = rows_of(c)
        for n in range(2):
            cols = slice(n * 256, (n + 1) * 256)
            ret = r_md[pair, :, c % 2, n * 16:(n + 1) * 16, :].reshape(256, T)
            a4[n] += dot(ret, g[rows, cols])
            lo[rows, cols] = dot(ret.T, w4p[n]).astype(BF16)
        return pair

    def first_part(c, n, ret):
        a1[n] += dot_nt(xt[c, n], ret)

    def tokens_part(c, n, ret):
        tg[rows_of(c), n * 256:(n + 1) * 256] = dot(ret.T, w1t[n]).astype(BF16)

    def back(r_b, c):
        return r_b[c // 2, :, c % 2].reshape(256, T)

    def in_stage(c, carry):
        ret = back(r_b0, c)
        first_part(c, 0, ret)
        tokens_part(c, 0, ret)
        return carry

    arrive(md_sem.at[0], r_md.at[0])
    lax.fori_loop(0, 2, out_stage, 0)
    arrive(b0_sem.at[0], r_b0.at[0])
    lax.fori_loop(0, 2, in_stage, 0)
    reduce_take(2, p3, o3)
    reduce_take(1, p2, o2)
    arrive(md_sem.at[1], r_md.at[1])
    lax.fori_loop(2, 4, out_stage, 1)
    for n in range(2):
        full = dot(pout, (a4[n] * scale).astype(BF16)).astype(BF16)
        for d in range(8):
            q4[d, n] = full[d * 32:(d + 1) * 32, :]
    reduce_send(3, q4, p4)
    arrive(b0_sem.at[1], r_b0.at[1])
    lax.fori_loop(2, 4, in_stage, 0)
    full = (a1[0] * scale).astype(BF16)
    for d in range(8):
        q0[d] = full[d * 32:(d + 1) * 32, :]
    reduce_send(4, q0, p0)
    arrive(b1_sem.at[0], r_b1.at[0])
    for c in range(2):
        first_part(c, 1, back(r_b1, c))
        tokens_part(c, 1, back(r_b1, c))
    reduce_take(3, p4, o4)
    reduce_take(4, p0, o1.at[0])
    arrive(b1_sem.at[1], r_b1.at[1])
    full = a1[1] + dot_nt(xt[2, 1], back(r_b1, 2)) + dot_nt(xt[3, 1], back(r_b1, 3))
    full = (full * scale).astype(BF16)
    for d in range(8):
        q1[d] = full[d * 32:(d + 1) * 32, :]
    reduce_send(0, q1, p1)
    for c in range(2, 4):
        tokens_part(c, 1, back(r_b1, c))
    for c in range(CHUNKS):
        sent(in_sem.at[c], s_in.at[c])
    for pair in range(2):
        sent(md_sem.at[pair], s_md.at[pair])
        sent(b0_sem.at[pair], s_b0.at[pair])
        sent(b1_sem.at[pair], s_b1.at[pair])
    for n, src in enumerate((q1, q2, q3, q4, q0)):
        reduce_sent(n, src)
    reduce_take(0, p1, o1.at[1])


def finish(*refs):
    sems = refs[-1]
    copies = [pltpu.make_async_copy(refs[n], refs[n + 6], sems.at[n]) for n in range(6)]
    for copy in copies:
        copy.start()
    for copy in copies:
        copy.wait()


def shards(scale, tokens, cotangent, first, second, third, fourth):
    rows = tokens.shape[0]
    T = rows // CHUNKS
    any_spec = pl.BlockSpec(memory_space=pl.ANY)
    shape = jax.ShapeDtypeStruct
    grads = [(2, 32, 256), (2, 32, 1024), (2, 128, 256), (2, 32, 256)]
    sums = [(32, 256), (32, 256)] + grads[1:]
    outs = [(tokens.shape, BF16), (tokens.shape, BF16)] + [(s, F32) for s in grads]
    parts = pl.pallas_call(
        functools.partial(kernel, scale),
        out_shape=[pltpu.VMEM(s, d) for s, d in outs],
        in_specs=[any_spec] * 6,
        out_specs=[pl.BlockSpec(memory_space=pltpu.VMEM)] * 6,
        scratch_shapes=[
            pltpu.VMEM(tokens.shape, BF16),
            pltpu.VMEM(tokens.shape, BF16),
            pltpu.VMEM(first.shape, BF16),
            pltpu.VMEM(second.shape, BF16),
            pltpu.VMEM(third.shape, BF16),
            pltpu.VMEM(fourth.shape, BF16),
            pltpu.VMEM((2, 256, 256), BF16),
            pltpu.VMEM((2, 256, 1024), BF16),
            pltpu.VMEM((2, 1024, 256), BF16),
            pltpu.VMEM((2, 256, 1024), BF16),
            pltpu.VMEM((2, 256, 256), BF16),
            pltpu.VMEM((CHUNKS, 2, 256, T), BF16),
            pltpu.VMEM((CHUNKS, 16, 2, 32, T), BF16),
            pltpu.VMEM((CHUNKS, 16, 2, 32, T), BF16),
            pltpu.VMEM((2, 16, 2, 32, T), BF16),
            pltpu.VMEM((2, 16, 2, 32, T), BF16),
            pltpu.VMEM((2, 16, 2, 16, T), BF16),
            pltpu.VMEM((2, 16, 2, 16, T), BF16),
            pltpu.VMEM((2, 16, 2, 16, T), BF16),
            pltpu.VMEM((2, 16, 2, 16, T), BF16),
            pltpu.VMEM((1024, T), BF16),
            pltpu.VMEM((1024, T), BF16),
            pltpu.VMEM((2, 256, T), F32),
            pltpu.VMEM((2, 256, T), F32),
            pltpu.VMEM((2, 256, 256), F32),
            pltpu.VMEM((2, 1024, 256), F32),
            pltpu.VMEM((2, 1024, 256), F32),
            pltpu.VMEM((2, 256, 256), F32),
        ]
        + [pltpu.VMEM((8,) + s, BF16) for s in sums] * 2
        + [
            pltpu.SemaphoreType.DMA((4,)),
            pltpu.SemaphoreType.DMA((CHUNKS,)),
            pltpu.SemaphoreType.DMA((CHUNKS,)),
            pltpu.SemaphoreType.DMA((CHUNKS, 2)),
            pltpu.SemaphoreType.DMA((2, 2)),
            pltpu.SemaphoreType.DMA((2, 2)),
            pltpu.SemaphoreType.DMA((2, 2)),
            pltpu.SemaphoreType.DMA((5,)),
            pltpu.SemaphoreType.DMA((5,)),
        ],
        compiler_params=pltpu.CompilerParams(
            collective_id=0, has_side_effects=True, vmem_limit_bytes=48 * 1024 * 1024
        ),
        cost_estimate=pl.CostEstimate(
            flops=16 * 10**9, bytes_accessed=12 * 2**20, transcendentals=4 * 2**20
        ),
    )(*(pltpu.with_memory_space_constraint(a, pltpu.HBM) for a in (tokens, cotangent, first, second, third, fourth)))
    return pl.pallas_call(
        finish,
        out_shape=[shape(s, d) for s, d in outs],
        in_specs=[pl.BlockSpec(memory_space=pltpu.VMEM)] * 6,
        out_specs=[any_spec] * 6,
        scratch_shapes=[pltpu.SemaphoreType.DMA((6,))],
        compiler_params=pltpu.CompilerParams(vmem_limit_bytes=1024 * 1024),
    )(*parts)


def solution(mesh):
    in_specs = (P("dp", "tensor"),) * 2 + (P("tensor", None, None),) * 4
    out_specs = (P("dp", "tensor"),) * 2 + (P("tensor", "dp", None),) * 4

    def run(tokens, *rest):
        scale = tokens.shape[0] ** -0.5
        step = jax.shard_map(
            functools.partial(shards, scale), mesh=mesh, in_specs=in_specs, out_specs=out_specs, check_vma=False
        )
        return step(tokens, *rest)

    return run
```
